256 devices in a mesh: ctx: 64 (over z, y, core), head: 4 (over x).
Axes of the slice: x: 4, y: 4, z: 8, core: 2. Of those that a mesh axis runs over, the one named last changes fastest.
Arguments:
- queries: bfloat16 [16384, 2048], P(('ctx', 'head')), may hold values from -150 to 150
- key_rows: bfloat16 [16384, 2048], P(('ctx', 'head')), may hold values from -7 to 7
- value_rows: bfloat16 [16384, 2048], P(('ctx', 'head')), may hold values from -6 to 6
- grad_output: bfloat16 [16384, 2048], P(('ctx', 'head')), may hold values from -6 to 6
- chosen_blocks: int32 [64, 3], replicated, may hold values from -1 to 62, as said below
Outputs:
- attended: bfloat16 [16384, 2048], P(('ctx', 'head'))
- grad_queries: bfloat16 [16384, 2048], P(('ctx', 'head'))
- grad_keys: bfloat16 [16384, 2048], P(('ctx', 'head'))
- grad_values: bfloat16 [16384, 2048], P(('ctx', 'head'))
The draws below stay inside these ranges and needn't reach their ends.
Inputs may be any that keep to these rules, and one draw needn't show every extreme that they name: Row b of chosen_blocks lists min(b, 3) different blocks below b, block b - 1 among them for every b >= 1, then -1 in the remaining places.
All inputs are finite; a program needn't handle non-finite values.
Results may differ from the reference program's by a relative error of at most 0.02.
Values may be sent and summed in bfloat16 or wider, within the bound.
A program may use at most 64 MiB of HBM per device.

```python
import jax
import jax.numpy as jnp
from jax import lax

HEADS = 16
HEAD_DIM = 128
TOPK = 3
BLOCK = 256
BLOCKS = 64
SEQ = 16384


def shared_keys(key):
    return jnp.clip(jax.random.normal(key, (SEQ, HEADS * HEAD_DIM), jnp.float32), -6.0, 6.0)


def draw_key_rows(key, part):
    base = shared_keys(key)
    return base.astype(jnp.bfloat16)


def draw_queries(key, part):
    base = shared_keys(key)
    key = jax.random.fold_in(key, 1)
    fresh = jnp.clip(jax.random.normal(key, base.shape, jnp.float32), -6.0, 6.0)
    return fresh.astype(jnp.bfloat16)


def draw_chosen_blocks(key, part):
    key = jax.random.fold_in(key, 3)
    row_ids = jnp.arange(BLOCKS)[:, None]
    col_ids = jnp.arange(BLOCKS)[None, :]
    noise = jax.random.randint(key, (BLOCKS, BLOCKS), 0, 4096)
    boost = jnp.where(col_ids == 0, 3000, 0) + jnp.where(col_ids == row_ids - 1, 5000, 0)
    score = (noise + boost) * BLOCKS + col_ids
    score = jnp.where(col_ids < row_ids, score, -1 - col_ids)
    top_vals, top_idx = lax.top_k(score, TOPK)
    return jnp.where(top_vals >= 0, top_idx, -1).astype(jnp.int32)


def steps_of(rng, shape, split, least, largest):
    gain = 1.0
    for dim, blocks in split:
        steps = jax.random.uniform(jax.random.fold_in(jax.random.fold_in(rng, 6), dim), (blocks,), jnp.float32, least / len(split), largest / len(split))
        gain = gain * jnp.repeat(jnp.exp(steps), shape[dim] // blocks).reshape((-1,) + (1,) * (len(shape) - 1 - dim))
    return gain


def gaussian(stream_key, extent, scale, most, split=(), held_as=jnp.bfloat16):
    result = jax.random.normal(stream_key, extent, jnp.float32) * scale
    if len(split) > 0:
        result = steps_of(stream_key, extent, split, -0.22, 0.18) * result
    return jnp.clip(result, min=-most, max=most).astype(held_as)


def setup_inputs(seed: int = 0) -> dict:
    splits = jax.random.split(jax.random.key(seed), 6)
    return {
        "queries": draw_queries(jax.random.fold_in(splits[5], 71), 0),
        "key_rows": draw_key_rows(jax.random.fold_in(splits[5], 71), 0),
        "value_rows": gaussian(splits[2], (SEQ, HEADS * HEAD_DIM), 1.0, 6.0, ((0, 256),)),
        "grad_output": gaussian(splits[3], (SEQ, HEADS * HEAD_DIM), 1.0, 6.0, ((0, 256),)),
        "chosen_blocks": draw_chosen_blocks(jax.random.fold_in(splits[5], 71), 0),
    }


def rounded(values):
    return lax.optimization_barrier(values.astype(jnp.bfloat16)).astype(jnp.float32)


def visible(usable):
    col_ids = jnp.arange((TOPK + 1) * BLOCK)
    row_ids = jnp.arange(BLOCK)
    slot_of = jnp.minimum(col_ids // BLOCK, TOPK - 1)
    panel_ok = jnp.any((slot_of[:, None] == jnp.arange(TOPK)[None, :]) & usable[None, :], axis=1)
    causal = (col_ids[None, :] - TOPK * BLOCK) <= row_ids[:, None]
    return jnp.where((col_ids < TOPK * BLOCK)[None, :], panel_ok[None, :], causal)


def reference(queries, key_rows, value_rows, grad_output, chosen_blocks):
    features = HEADS * HEAD_DIM
    scaling = HEAD_DIM ** -0.5
    highest = lax.Precision.HIGHEST
    q_all = queries.astype(jnp.float32).reshape(BLOCKS, BLOCK, HEADS, HEAD_DIM)
    k_all = key_rows.astype(jnp.float32).reshape(BLOCKS, BLOCK, HEADS, HEAD_DIM)
    v_all = value_rows.astype(jnp.float32).reshape(BLOCKS, BLOCK, HEADS, HEAD_DIM)
    g_all = grad_output.astype(jnp.float32).reshape(BLOCKS, BLOCK, HEADS, HEAD_DIM)

    def block_step(totals, block_id):
        key_grad, value_grad = totals
        picked = chosen_blocks[block_id]
        usable = picked >= 0
        clamped = jnp.maximum(picked, 0).astype(jnp.int32)
        key_set = jnp.concatenate([k_all[clamped].reshape(TOPK * BLOCK, HEADS, HEAD_DIM), k_all[block_id]], axis=0)
        value_set = jnp.concatenate([v_all[clamped].reshape(TOPK * BLOCK, HEADS, HEAD_DIM), v_all[block_id]], axis=0)
        q_block = q_all[block_id]
        g_block = g_all[block_id]
        allowed = visible(usable)
        scores = jnp.einsum("qhd,khd->hqk", q_block, key_set, precision=highest) * scaling
        scores = jnp.where(allowed[None], scores, -jnp.inf)
        peak = jnp.max(scores, axis=2, keepdims=True)
        log_total = peak + jnp.log(jnp.sum(jnp.exp(scores - peak), axis=2, keepdims=True))
        attend = jnp.exp(scores - log_total)
        attend_b = rounded(attend)
        out_block = jnp.einsum("hqk,khd->qhd", attend_b, value_set, precision=highest).astype(jnp.bfloat16)
        grad_prob = jnp.einsum("qhd,khd->hqk", g_block, value_set, precision=highest)
        row_dot = jnp.transpose(jnp.sum(g_block * out_block.astype(jnp.float32), axis=2))[:, :, None]
        grad_score = rounded(attend * (grad_prob - row_dot))
        grad_query = (jnp.einsum("hqk,khd->qhd", grad_score, key_set, precision=highest) * scaling).astype(jnp.bfloat16)
        grad_key = jnp.einsum("hqk,qhd->khd", grad_score, q_block, precision=highest).reshape((TOPK + 1) * BLOCK, features) * scaling
        grad_value = jnp.einsum("hqk,qhd->khd", attend_b, g_block, precision=highest).reshape((TOPK + 1) * BLOCK, features)
        weight = jnp.where(usable, 1.0, 0.0).astype(grad_key.dtype)[:, None, None]
        key_grad = key_grad.at[clamped].add(grad_key[: TOPK * BLOCK].reshape(TOPK, BLOCK, features) * weight)
        key_grad = key_grad.at[block_id].add(grad_key[TOPK * BLOCK:])
        value_grad = value_grad.at[clamped].add(grad_value[: TOPK * BLOCK].reshape(TOPK, BLOCK, features) * weight)
        value_grad = value_grad.at[block_id].add(grad_value[TOPK * BLOCK:])
        return (key_grad, value_grad), (out_block.reshape(BLOCK, features), grad_query.reshape(BLOCK, features))

    empty_grad = jnp.zeros((BLOCKS, BLOCK, features), jnp.float32)
    (key_grad, value_grad), (out_rows, dq_rows) = lax.scan(block_step, (empty_grad, empty_grad), jnp.arange(BLOCKS).astype(jnp.int32))
    return (out_rows.reshape(SEQ, features), dq_rows.reshape(SEQ, features),
            key_grad.reshape(SEQ, features).astype(jnp.bfloat16), value_grad.reshape(SEQ, features).astype(jnp.bfloat16))
```

```python
import functools

import jax
import jax.numpy as jnp
from jax import lax
from jax.experimental import pallas as pl
from jax.experimental.pallas import tpu as pltpu
from jax.sharding import PartitionSpec as P

MESH = pl.DeviceIdType.MESH
HEAD_DIM = 128
BLOCKS = 64
GROUP = 4
SLOTS = 13
PLACES = 16
ROWS = 16
BLOCK = 256
SCALE = HEAD_DIM**-0.5
LOG2E = 1.4426950408889634
BF16 = jnp.bfloat16
F32 = jnp.float32

NT = (((1,), (1,)), ((), ()))
NN = (((1,), (0,)), ((), ()))
TN = (((0,), (0,)), ((), ()))


def dot(a, b, dims):
    return lax.dot_general(a, b, dims, preferred_element_type=F32)


def kernel(
    q_in, k_in, v_in, g_in, chosen,
    o_out, dq_out, dk_out, dv_out,
    k_stripes, v_stripes, k_send, v_send, k_got, v_got, q_blk, g_blk, probs,
    o_blk, dq_blk, dk_send, dv_send, dk_got, dv_got, spread, dk_sum, dv_sum, carry, table,
    stripe_send, stripe_recv, pick_send, pick_recv, head_send, head_recv,
    back_send, back_recv, sum_send, sum_recv, home_send, home_recv,
):
    ctx = lax.axis_index("ctx")
    x = lax.axis_index("head")
    z = lax.div(ctx, 8)
    y = lax.rem(lax.div(ctx, 2), 4)
    c = lax.rem(ctx, 2)
    head = 2 * z + c
    place = 4 * x + y

    def group_at(px, py):
        low = lax.rem(px + 8 - z, 4)
        high = lax.rem(py + 8 - lax.div(z, 2), 4)
        return 4 * high + low

    group = group_at(x, y)

    barrier = pltpu.get_barrier_semaphore()

    def greet(o, _):
        pl.semaphore_signal(
            barrier, inc=1, device_id=(lax.rem(ctx + o, BLOCKS), x), device_id_type=MESH
        )
        return 0

    lax.fori_loop(1, BLOCKS, greet, 0)

    def place_id(p):
        return (8 * z + 2 * lax.rem(p, 4) + c, lax.div(p, 4))

    def greet_place(o, _):
        p = lax.rem(place + o, PLACES)

        @pl.when(lax.div(p, 4) != x)
        def _():
            pl.semaphore_signal(barrier, inc=1, device_id=place_id(p), device_id_type=MESH)

        return 0

    lax.fori_loop(1, PLACES, greet_place, 0)
    pl.semaphore_wait(barrier, BLOCKS - 1 + 12)

    def stripe_src(ref, t):
        t_y = lax.rem(lax.div(t, 2), 4)
        t_head = 2 * lax.div(t, 8) + lax.rem(t, 2)
        return ref.at[
            pl.ds(pl.multiple_of(t_y * ROWS, ROWS), ROWS),
            pl.ds(pl.multiple_of(t_head * HEAD_DIM, HEAD_DIM), HEAD_DIM),
        ]

    def send_stripes(src, dst, n):
        def step(o, _):
            t = lax.rem(ctx + o, BLOCKS)
            pltpu.make_async_remote_copy(
                src_ref=stripe_src(src, t),
                dst_ref=dst.at[ctx],
                send_sem=stripe_send.at[n],
                recv_sem=stripe_recv.at[n],
                device_id=(t, x),
                device_id_type=MESH,
            ).start()
            return 0

        lax.fori_loop(1, BLOCKS, step, 0)
        pltpu.make_async_copy(stripe_src(src, ctx), dst.at[ctx], stripe_recv.at[n]).start()

    def wait_all(ref, sem):
        pltpu.make_async_copy(ref, ref, sem).wait()

    send_stripes(k_in, k_stripes, 0)
    send_stripes(v_in, v_stripes, 1)

    def fill_table(p, _):
        g = group_at(lax.div(p, 4), lax.rem(p, 4))
        base = p * SLOTS
        for i in range(GROUP):
            b = 4 * g + i
            e0, e1, e2 = chosen[b, 0], chosen[b, 1], chosen[b, 2]
            table[base + 3 * i] = b - 1
            table[base + 3 * i + 1] = jnp.where(e0 == b - 1, e1, e0)
            table[base + 3 * i + 2] = jnp.where(e2 == b - 1, e1, e2)
        table[base + 12] = 4 * g + 3
        return 0

    lax.fori_loop(0, PLACES, fill_table, 0)

    def group_copy(n, e, src, dst, away):
        e_z, e_c = lax.div(e, 2), lax.rem(e, 2)
        g = lax.div(ctx, 4)
        t_x = lax.rem(g + e_z, 4)
        t_y = lax.rem(lax.div(g, 4) + lax.div(e_z, 2), 4)
        t = 8 * e_z + 2 * t_y + e_c
        here = jnp.logical_and(t == ctx, t_x == x)
        s = src.at[:, pl.ds(pl.multiple_of(e * HEAD_DIM, HEAD_DIM), HEAD_DIM)]
        d = dst.at[
            pl.ds(pl.multiple_of(lax.rem(ctx, 4) * BLOCK + x * 64, 64), 64), :
        ]
        both(n, e, s, d, (t, t_x), here, away)

    def home_copy(n, e, src, dst, away):
        i, t_x = lax.div(e, 4), lax.rem(e, 4)
        t = 4 * group + i
        here = jnp.logical_and(t == ctx, t_x == x)
        s = src.at[pl.ds(pl.multiple_of(i * BLOCK + t_x * 64, 64), 64), :]
        d = dst.at[:, pl.ds(pl.multiple_of(head * HEAD_DIM, HEAD_DIM), HEAD_DIM)]
        both(n, e, s, d, (t, t_x), here, away)

    def both(n, e, s, d, t, here, away):
        def remote():
            return pltpu.make_async_remote_copy(
                src_ref=s, dst_ref=d, send_sem=head_send.at[n, e], recv_sem=head_recv.at[n],
                device_id=t, device_id_type=MESH,
            )

        @pl.when(jnp.logical_not(here))
        def _():
            if away:
                remote().start()
            else:
                remote().wait_send()

        if away:
            @pl.when(here)
            def _():
                pltpu.make_async_copy(s, d, head_recv.at[n]).start()

    def each(lo, hi, fn):
        def step(e, _):
            fn(e)
            return 0

        lax.fori_loop(lo, hi, step, 0)

    def send_picks(stripes, out, got, n):
        def step(o, _):
            p = lax.rem(place + o, PLACES)
            for s in range(SLOTS):
                out[p, s] = stripes[jnp.maximum(table[p * SLOTS + s], 0)]
            pltpu.make_async_remote_copy(
                src_ref=out.at[p],
                dst_ref=got.at[place],
                send_sem=pick_send.at[n],
                recv_sem=pick_recv.at[n],
                device_id=place_id(p),
                device_id_type=MESH,
            ).start()
            return 0

        lax.fori_loop(1, PLACES, step, 0)
        for s in range(SLOTS):
            got[place, s] = stripes[jnp.maximum(table[place * SLOTS + s], 0)]

    wait_all(k_stripes, stripe_recv.at[0])
    send_picks(k_stripes, k_send, k_got, 0)
    each(0, PLACES, lambda e: group_copy(0, e, q_in, q_blk, True))
    wait_all(v_stripes, stripe_recv.at[1])
    send_picks(v_stripes, v_send, v_got, 1)
    each(0, PLACES, lambda e: group_copy(1, e, g_in, g_blk, True))

    def block_of(ref, s):
        return ref[:, s].reshape(BLOCK, HEAD_DIM)

    def rows_of(i):
        return pl.ds(pl.multiple_of(i * BLOCK, BLOCK), BLOCK)

    wait_all(q_blk, head_recv.at[0])
    wait_all(k_got.at[pl.ds(0, PLACES - 1)], pick_recv.at[0])

    def soft(i):
        qi = q_blk[rows_of(i), :]
        b = 4 * group + i
        d0 = table[place * SLOTS + 3 * i + 1]
        d1 = table[place * SLOTS + 3 * i + 2]
        keys = lax.broadcasted_iota(jnp.int32, (BLOCK, BLOCK), 0)
        asks = lax.broadcasted_iota(jnp.int32, (BLOCK, BLOCK), 1)
        scores = []
        for s in range(4):
            raw = dot(block_of(k_got, 3 * i + s), qi, NT)
            if s == 3:
                raw = jnp.where(keys <= asks, raw, -jnp.inf)
            else:
                usable = (b, d0 + 1, d1 + 1)[s] > 0
                raw = raw + jnp.where(usable, 0.0, -jnp.inf).astype(F32)
            scores.append(raw)
        peak = functools.reduce(
            jnp.maximum, [jnp.max(r, axis=0, keepdims=True) for r in scores]
        )
        powers = [jnp.exp2((r - peak) * (SCALE * LOG2E)) for r in scores]
        total = functools.reduce(
            jnp.add, [jnp.sum(r, axis=0, keepdims=True) for r in powers]
        )
        inverse = 1.0 / total
        for s in range(4):
            probs[i, s] = (powers[s] * inverse).astype(BF16)

    each(0, GROUP, soft)

    def put(ref, s, value):
        ref[:, s] = value.astype(BF16).reshape(PLACES, ROWS, HEAD_DIM)

    def send_back(src, dst, n, lo, hi):
        def step(o, _):
            p = lax.rem(place + o, PLACES)
            pltpu.make_async_remote_copy(
                src_ref=src.at[p, pl.ds(lo, hi - lo)],
                dst_ref=dst.at[place, pl.ds(lo, hi - lo)],
                send_sem=back_send.at[n],
                recv_sem=back_recv.at[n],
                device_id=place_id(p),
                device_id_type=MESH,
            ).start()
            return 0

        lax.fori_loop(1, PLACES, step, 0)
        pltpu.make_async_copy(
            src.at[place, pl.ds(lo, hi - lo)], dst.at[place, pl.ds(lo, hi - lo)], back_recv.at[n]
        ).start()

    wait_all(g_blk, head_recv.at[1])
    carry[...] = jnp.zeros_like(carry)

    def value_grads(i):
        gi = g_blk[rows_of(i), :]
        for s in range(4):
            dv = dot(probs[i, s], gi, NN)
            if s == 0:
                put(dv_send, 3 * i, dv + carry[0])
            elif s < 3:
                put(dv_send, 3 * i + s, dv)
            else:
                carry[0] = dv

    each(0, GROUP, value_grads)
    put(dv_send, SLOTS - 1, carry[0])
    send_back(dv_send, dv_got, 0, 0, SLOTS)

    wait_all(v_got.at[pl.ds(0, PLACES - 1)], pick_recv.at[1])

    def score_grads(i):
        qi = q_blk[rows_of(i), :]
        gi = g_blk[rows_of(i), :]
        ot = functools.reduce(
            jnp.add, [dot(block_of(v_got, 3 * i + s), probs[i, s], TN) for s in range(4)]
        )
        out = ot.T.astype(BF16)
        o_blk[rows_of(i), :] = out
        row_dot = jnp.sum(
            gi.astype(F32).T * ot.astype(BF16).astype(F32), axis=0, keepdims=True
        )
        dqt = jnp.zeros((HEAD_DIM, BLOCK), F32)
        for s in range(4):
            dp = dot(block_of(v_got, 3 * i + s), gi, NT)
            ds = (probs[i, s].astype(F32) * (dp - row_dot)).astype(BF16)
            dqt = dqt + dot(block_of(k_got, 3 * i + s), ds, TN)
            dk = dot(ds, qi, NN) * SCALE
            if s == 0:
                put(dk_send, 3 * i, dk + carry[1])
            elif s < 3:
                put(dk_send, 3 * i + s, dk)
            else:
                carry[1] = dk
        dq_blk[rows_of(i), :] = (dqt * SCALE).T.astype(BF16)

    each(0, 2, score_grads)
    send_back(dk_send, dk_got, 1, 0, 6)
    each(2, GROUP, score_grads)
    put(dk_send, SLOTS - 1, carry[1])
    send_back(dk_send, dk_got, 1, 6, SLOTS)
    each(0, PLACES, lambda e: home_copy(2, e, o_blk, o_out, True))
    each(0, PLACES, lambda e: home_copy(3, e, dq_blk, dq_out, True))

    lanes = lax.broadcasted_iota(jnp.int32, (1, 128), 1)

    def spread_chunk(k):
        target = jnp.full((1, 128), -1, jnp.int32)
        for j in range(8):
            row = table[8 * k + j] * ROWS
            target = jnp.where(lax.div(lanes, 16) == j, row, target)
        target = target + lax.rem(lanes, 16)
        rows = lax.broadcasted_iota(jnp.int32, (BLOCKS * ROWS, 128), 0)
        spread[k] = jnp.where(rows == target, 1.0, 0.0).astype(BF16)

    each(0, PLACES * SLOTS // 8, spread_chunk)

    def sum_up(got, total, n, out):
        wait_all(got, back_recv.at[n])
        acc = jnp.zeros((BLOCKS * ROWS, HEAD_DIM), F32)
        terms = got[...].reshape(PLACES * SLOTS * ROWS, HEAD_DIM)
        wide = jnp.concatenate([spread[k] for k in range(PLACES * SLOTS // 8)], axis=1)
        acc = dot(wide, terms, NN)
        total[...] = acc.astype(BF16).reshape(BLOCKS, ROWS, HEAD_DIM)
        dst = out.at[
            pl.ds(pl.multiple_of(y * ROWS, ROWS), ROWS),
            pl.ds(pl.multiple_of(head * HEAD_DIM, HEAD_DIM), HEAD_DIM),
        ]

        def step(o, _):
            t = lax.rem(ctx + o, BLOCKS)
            pltpu.make_async_remote_copy(
                src_ref=total.at[t],
                dst_ref=dst,
                send_sem=sum_send.at[n],
                recv_sem=sum_recv.at[n],
                device_id=(t, x),
                device_id_type=MESH,
            ).start()
            return 0

        lax.fori_loop(1, BLOCKS, step, 0)
        pltpu.make_async_copy(total.at[ctx], dst, sum_recv.at[n]).start()

    sum_up(dv_got, dv_sum, 0, dv_out)
    sum_up(dk_got, dk_sum, 1, dk_out)

    for n, ref in ((0, k_stripes), (1, v_stripes)):
        wait_all(ref.at[pl.ds(0, BLOCKS - 1)], stripe_send.at[n])
    for n, ref in ((0, k_send), (1, v_send)):
        wait_all(ref.at[pl.ds(0, PLACES - 1)], pick_send.at[n])
    for n, ref in ((0, dv_send), (1, dk_send)):
        wait_all(ref.at[pl.ds(0, PLACES - 1)], back_send.at[n])
    each(0, PLACES, lambda e: group_copy(0, e, q_in, q_blk, False))
    each(0, PLACES, lambda e: group_copy(1, e, g_in, g_blk, False))
    each(0, PLACES, lambda e: home_copy(2, e, o_blk, o_out, False))
    each(0, PLACES, lambda e: home_copy(3, e, dq_blk, dq_out, False))
    wait_all(o_out, head_recv.at[2])
    wait_all(dq_out, head_recv.at[3])
    for n, ref, out in ((0, dv_sum, dv_out), (1, dk_sum, dk_out)):
        wait_all(ref.at[pl.ds(0, BLOCKS - 1)], sum_send.at[n])
        wait_all(out, sum_recv.at[n])


def per_device(queries, key_rows, value_rows, grad_output, chosen_blocks):
    vmem = pl.BlockSpec(memory_space=pltpu.VMEM)
    shape = jax.ShapeDtypeStruct(queries.shape, BF16)
    dma = pltpu.SemaphoreType.DMA
    stripes = pltpu.VMEM((BLOCKS, ROWS, HEAD_DIM), BF16)
    picks = pltpu.VMEM((PLACES, SLOTS, ROWS, HEAD_DIM), BF16)
    rows = pltpu.VMEM((GROUP * BLOCK, HEAD_DIM), BF16)
    return pl.pallas_call(
        kernel,
        out_shape=(shape,) * 4,
        in_specs=[vmem] * 4 + [pl.BlockSpec(memory_space=pltpu.SMEM)],
        out_specs=(vmem,) * 4,
        scratch_shapes=[
            stripes, stripes, picks, picks, picks, picks, rows, rows,
            pltpu.VMEM((GROUP, 4, BLOCK, BLOCK), BF16),
            rows, rows, picks, picks, picks, picks,
            pltpu.VMEM((PLACES * SLOTS // 8, BLOCKS * ROWS, 128), BF16),
            stripes, stripes,
            pltpu.VMEM((2, BLOCK, HEAD_DIM), F32),
            pltpu.SMEM((PLACES * SLOTS,), jnp.int32),
            dma((2,)), dma((2,)), dma((2,)), dma((2,)), dma((4, PLACES)), dma((4,)),
            dma((2,)), dma((2,)), dma((2,)), dma((2,)), dma((2,)), dma((2,)),
        ],
        compiler_params=pltpu.CompilerParams(
            collective_id=0, has_side_effects=True, vmem_limit_bytes=56 * 2**20
        ),
    )(queries, key_rows, value_rows, grad_output, chosen_blocks)


def solution(mesh):
    placed = P(("ctx", "head"), None)
    return jax.shard_map(
        per_device,
        mesh=mesh,
        in_specs=(placed,) * 4 + (P(),),
        out_specs=(placed,) * 4,
        check_vma=False,
    )
```

```python
import functools

import jax
import jax.numpy as jnp
from jax import lax
from jax.experimental import pallas as pl
from jax.experimental.pallas import tpu as pltpu
from jax.sharding import PartitionSpec as P

MESH = pl.DeviceIdType.MESH
HEAD_DIM = 128
BLOCKS = 64
GROUP = 4
SLOTS = 13
PLACES = 16
ROWS = 16
BLOCK = 256
SCALE = HEAD_DIM**-0.5
LOG2E = 1.4426950408889634
BF16 = jnp.bfloat16
F32 = jnp.float32

NT = (((1,), (1,)), ((), ()))
NN = (((1,), (0,)), ((), ()))
TN = (((0,), (0,)), ((), ()))


def dot(a, b, dims):
    return lax.dot_general(a, b, dims, preferred_element_type=F32)


def kernel(
    q_in, k_in, v_in, g_in, chosen,
    o_out, dq_out, dk_out, dv_out,
    k_stripes, v_stripes, k_send, v_send, k_got, v_got, q_mid, g_mid, q_blk, g_blk, probs,
    o_blk, dq_blk, o_mid, dq_mid, dk_send, dv_send, dk_got, dv_got, spread, dk_sum, dv_sum, carry, row_dots, table,
    stripe_send, stripe_recv, pick_send, pick_recv, head_send, head_recv,
    back_send, back_recv, sum_send, sum_recv, home_send, home_recv,
):
    ctx = lax.axis_index("ctx")
    x = lax.axis_index("head")
    z = lax.div(ctx, 8)
    y = lax.rem(lax.div(ctx, 2), 4)
    c = lax.rem(ctx, 2)
    head = 2 * z + c
    place = 4 * x + y

    def group_at(px, py):
        odd, px_low, py_low = lax.div(px, 2), lax.rem(px, 2), lax.rem(py, 2)
        low = (1 - odd) * px_low + odd * lax.rem(py_low + z, 2)
        high = (1 - odd) * lax.rem(py_low + c, 2) + odd * lax.rem(px_low + c, 2)
        return 2 * lax.rem(z + 4 * high + 2 * low + odd, 8) + lax.div(py, 2)

    def place_of(g, e_z, e_c):
        offset = lax.rem(lax.div(g, 2) + 8 - e_z, 8)
        odd, d = lax.rem(offset, 2), lax.div(offset, 2)
        high = lax.rem(lax.div(d, 2) + e_c, 2)
        even_place = 2 * lax.rem(d, 2) + high
        odd_place = 4 + 2 * high + lax.rem(d + e_z, 2)
        t = (1 - odd) * even_place + odd * odd_place
        return lax.div(t, 2), 2 * lax.rem(g, 2) + lax.rem(t, 2)

    group = group_at(x, y)

    def head_z(e_c):
        odd, px_low, py_low = lax.div(x, 2), lax.rem(x, 2), lax.rem(y, 2)
        low = (1 - odd) * px_low + odd * lax.rem(py_low + z + 1, 2)
        high = (1 - odd) * lax.rem(py_low + e_c, 2) + odd * lax.rem(px_low + e_c, 2)
        return lax.rem(z + 8 - (4 * high + 2 * low + odd), 8)

    barrier = pltpu.get_barrier_semaphore()

    def greet(o, _):
        pl.semaphore_signal(
            barrier, inc=1, device_id=(lax.rem(ctx + o, BLOCKS), x), device_id_type=MESH
        )
        return 0

    lax.fori_loop(1, BLOCKS, greet, 0)

    def place_id(p):
        return (8 * z + 2 * lax.rem(p, 4) + c, lax.div(p, 4))

    def greet_place(o, _):
        p = lax.rem(place + o, PLACES)

        @pl.when(lax.div(p, 4) != x)
        def _():
            pl.semaphore_signal(barrier, inc=1, device_id=place_id(p), device_id_type=MESH)

        return 0

    lax.fori_loop(1, PLACES, greet_place, 0)
    pl.semaphore_wait(barrier, BLOCKS - 1 + 12)

    def each(lo, hi, fn):
        def step(e, _):
            fn(e)
            return 0

        lax.fori_loop(lo, hi, step, 0)

    def stripe_src(ref, t):
        t_y = lax.rem(lax.div(t, 2), 4)
        t_head = 2 * lax.div(t, 8) + lax.rem(t, 2)
        return ref.at[
            pl.ds(pl.multiple_of(t_y * ROWS, ROWS), ROWS),
            pl.ds(pl.multiple_of(t_head * HEAD_DIM, HEAD_DIM), HEAD_DIM),
        ]

    def send_stripes(src, dst, n, beside):
        def stripe(o):
            t = lax.rem(ctx + o, BLOCKS)
            pltpu.make_async_remote_copy(
                src_ref=stripe_src(src, t),
                dst_ref=dst.at[ctx],
                send_sem=stripe_send.at[n],
                recv_sem=stripe_recv.at[n],
                device_id=(t, x),
                device_id_type=MESH,
            ).start()

        def step(e, _):
            for o in range(4):
                stripe(4 * e + o)
            beside(e)
            return 0

        for o in range(1, 4):
            stripe(o)
        beside(0)
        lax.fori_loop(1, PLACES, step, 0)
        pltpu.make_async_copy(stripe_src(src, ctx), dst.at[ctx], stripe_recv.at[n]).start()

    def wait_all(ref, sem):
        pltpu.make_async_copy(ref, ref, sem).wait()

    def turned(o):
        return lax.rem(head + o, PLACES)

    def one(n, e, s, d, t, here, mode):
        def remote():
            return pltpu.make_async_remote_copy(
                src_ref=s, dst_ref=d, send_sem=head_send.at[n, e], recv_sem=head_recv.at[n],
                device_id=t, device_id_type=MESH,
            )

        @pl.when(jnp.logical_not(here))
        def _():
            if mode:
                remote().start()
            else:
                remote().wait_send()

        if mode:

            @pl.when(here)
            def _():
                pltpu.make_async_copy(s, d, head_recv.at[n]).start()

    def columns(e):
        return pl.ds(pl.multiple_of(e * HEAD_DIM, HEAD_DIM), HEAD_DIM)

    def to_place(n, e, src, mid, mode=True):
        t_x, t_y = place_of(lax.div(ctx, 4), lax.div(e, 2), lax.rem(e, 2))
        here = jnp.logical_and(t_x == x, t_y == y)
        start = (2 * lax.rem(e, 2) + lax.rem(y, 2)) * BLOCK + x * 64
        one(
            n, e, src.at[:, columns(e)], mid.at[pl.ds(pl.multiple_of(start, 64), 64), :],
            (8 * z + 2 * t_y + c, t_x), here, mode,
        )

    def half_of(ref, j):
        return ref.at[pl.ds(pl.multiple_of(j * 2 * BLOCK, 2 * BLOCK), 2 * BLOCK), :]

    def to_head(n, j, mid, dst, mode=True):
        e_z = head_z(j)
        here = jnp.logical_and(e_z == z, c == j)
        one(n, j, half_of(mid, j), half_of(dst, c), (8 * e_z + 2 * y + j, x), here, mode)

    def from_head(n, j, src, mid, mode=True):
        t_z = lax.div(group, 2)
        here = jnp.logical_and(t_z == z, c == j)
        one(n, j, half_of(src, j), half_of(mid, c), (8 * t_z + 2 * y + j, x), here, mode)

    def from_place(n, e, mid, out, mode=True):
        j, low, t_x = lax.div(e, 8), lax.rem(lax.div(e, 4), 2), lax.rem(e, 4)
        t_y = 2 * lax.div(y, 2) + low
        here = jnp.logical_and(t_x == x, t_y == y)
        start = (2 * j + low) * BLOCK + t_x * 64
        one(
            n, e, mid.at[pl.ds(pl.multiple_of(start, 64), 64), :],
            out.at[:, columns(2 * head_z(j) + j)], (8 * z + 2 * t_y + c, t_x), here, mode,
        )

    send_stripes(k_in, k_stripes, 0, lambda e: to_place(0, turned(e), q_in, q_mid))
    send_stripes(v_in, v_stripes, 1, lambda e: to_place(1, turned(e), g_in, g_mid))

    def fill_table(p, _):
        g = group_at(lax.div(p, 4), lax.rem(p, 4))
        base = p * SLOTS
        for i in range(GROUP):
            b = 4 * g + i
            e0, e1, e2 = chosen[b, 0], chosen[b, 1], chosen[b, 2]
            table[base + 3 * i] = b - 1
            table[base + 3 * i + 1] = jnp.where(e0 == b - 1, e1, e0)
            table[base + 3 * i + 2] = jnp.where(e2 == b - 1, e1, e2)
        table[base + 12] = 4 * g + 3
        return 0

    lax.fori_loop(0, PLACES, fill_table, 0)

    def send_picks(stripes, out, got, n, beside):
        def step(o, _):
            p = lax.rem(place + o, PLACES)
            for s in range(SLOTS):
                out[p, s] = stripes[jnp.maximum(table[p * SLOTS + s], 0)]
            pltpu.make_async_remote_copy(
                src_ref=out.at[p],
                dst_ref=got.at[place],
                send_sem=pick_send.at[n],
                recv_sem=pick_recv.at[n],
                device_id=place_id(p),
                device_id_type=MESH,
            ).start()
            return 0

        lax.fori_loop(1, 5, step, 0)
        beside()
        lax.fori_loop(5, PLACES, step, 0)
        for s in range(SLOTS):
            got[place, s] = stripes[jnp.maximum(table[place * SLOTS + s], 0)]

    wait_all(k_stripes, stripe_recv.at[0])
    def head_part(n, mid, dst):
        wait_all(mid, head_recv.at[n])
        for j in range(2):
            to_head(n + 2, j, mid, dst)

    send_picks(k_stripes, k_send, k_got, 0, lambda: head_part(0, q_mid, q_blk))
    wait_all(v_stripes, stripe_recv.at[1])
    send_picks(v_stripes, v_send, v_got, 1, lambda: head_part(1, g_mid, g_blk))

    lanes = lax.broadcasted_iota(jnp.int32, (1, 128), 1)

    def spread_chunk(k):
        target = jnp.full((1, 128), -1, jnp.int32)
        for j in range(8):
            row = table[8 * k + j] * ROWS
            target = jnp.where(lax.div(lanes, 16) == j, row, target)
        target = target + lax.rem(lanes, 16)
        rows = lax.broadcasted_iota(jnp.int32, (BLOCKS * ROWS, 128), 0)
        spread[k] = jnp.where(rows == target, 1.0, 0.0).astype(BF16)

    each(0, PLACES * SLOTS // 8, spread_chunk)

    def block_of(ref, s):
        return ref[:, s].reshape(BLOCK, HEAD_DIM)

    def rows_of(i):
        at = 2 * lax.rem(i, 2) + lax.div(i, 2)
        return pl.ds(pl.multiple_of(at * BLOCK, BLOCK), BLOCK)

    wait_all(q_blk, head_recv.at[2])
    wait_all(k_got.at[pl.ds(0, PLACES - 1)], pick_recv.at[0])

    def soft(i):
        qi = q_blk[rows_of(i), :]
        b = 4 * group + i
        d0 = table[place * SLOTS + 3 * i + 1]
        d1 = table[place * SLOTS + 3 * i + 2]
        keys = lax.broadcasted_iota(jnp.int32, (BLOCK, BLOCK), 0)
        asks = lax.broadcasted_iota(jnp.int32, (BLOCK, BLOCK), 1)
        scores = []
        for s in range(4):
            raw = dot(block_of(k_got, 3 * i + s), qi, NT)
            if s == 3:
                raw = jnp.where(keys <= asks, raw, -jnp.inf)
            else:
                usable = (b, d0 + 1, d1 + 1)[s] > 0
                raw = raw + jnp.where(usable, 0.0, -jnp.inf).astype(F32)
            scores.append(raw)
        peak = functools.reduce(
            jnp.maximum, [jnp.max(r, axis=0, keepdims=True) for r in scores]
        )
        powers = [jnp.exp2((r - peak) * (SCALE * LOG2E)) for r in scores]
        total = functools.reduce(
            jnp.add, [jnp.sum(r, axis=0, keepdims=True) for r in powers]
        )
        inverse = 1.0 / total
        for s in range(4):
            probs[i, s] = (powers[s] * inverse).astype(BF16)

    each(0, GROUP, soft)

    def put(ref, s, value):
        ref[:, s] = value.astype(BF16).reshape(PLACES, ROWS, HEAD_DIM)

    def send_back(src, dst, n, lo, hi):
        def step(o, _):
            p = lax.rem(place + o, PLACES)
            pltpu.make_async_remote_copy(
                src_ref=src.at[p, pl.ds(lo, hi - lo)],
                dst_ref=dst.at[place, pl.ds(lo, hi - lo)],
                send_sem=back_send.at[n],
                recv_sem=back_recv.at[n],
                device_id=place_id(p),
                device_id_type=MESH,
            ).start()
            return 0

        lax.fori_loop(1, PLACES, step, 0)
        pltpu.make_async_copy(
            src.at[place, pl.ds(lo, hi - lo)], dst.at[place, pl.ds(lo, hi - lo)], back_recv.at[n]
        ).start()

    wait_all(g_blk, head_recv.at[3])
    carry[...] = jnp.zeros_like(carry)

    def value_grads(i):
        gi = g_blk[rows_of(i), :]
        for s in range(4):
            dv = dot(probs[i, s], gi, NN)
            if s == 0:
                put(dv_send, 3 * i, dv + carry[0])
            elif s < 3:
                put(dv_send, 3 * i + s, dv)
            else:
                carry[0] = dv

    each(0, 2, value_grads)
    send_back(dv_send, dv_got, 0, 0, 6)
    each(2, GROUP, value_grads)
    put(dv_send, SLOTS - 1, carry[0])
    send_back(dv_send, dv_got, 0, 6, SLOTS)

    wait_all(v_got.at[pl.ds(0, PLACES - 1)], pick_recv.at[1])

    def outputs(i):
        ot = functools.reduce(
            jnp.add, [dot(block_of(v_got, 3 * i + s), probs[i, s], TN) for s in range(4)]
        )
        out = ot.astype(BF16).astype(F32)
        o_blk[rows_of(i), :] = out.T.astype(BF16)
        row_dots[i] = jnp.sum(g_blk[rows_of(i), :].astype(F32).T * out, axis=0, keepdims=True)

    def score_grads(i):
        qi = q_blk[rows_of(i), :]
        gi = g_blk[rows_of(i), :]
        row_dot = row_dots[i]
        dqt = jnp.zeros((HEAD_DIM, BLOCK), F32)
        for s in range(4):
            dp = dot(block_of(v_got, 3 * i + s), gi, NT)
            ds = (probs[i, s].astype(F32) * (dp - row_dot)).astype(BF16)
            dqt = dqt + dot(block_of(k_got, 3 * i + s), ds, TN)
            dk = dot(ds, qi, NN) * SCALE
            if s == 0:
                put(dk_send, 3 * i, dk + carry[1])
            elif s < 3:
                put(dk_send, 3 * i + s, dk)
            else:
                carry[1] = dk
        dq_blk[rows_of(i), :] = (dqt * SCALE).T.astype(BF16)

    each(0, GROUP, outputs)
    for j in range(2):
        from_head(4, j, o_blk, o_mid)
    each(0, 2, score_grads)
    send_back(dk_send, dk_got, 1, 0, 6)
    each(2, GROUP, score_grads)
    put(dk_send, SLOTS - 1, carry[1])
    send_back(dk_send, dk_got, 1, 6, SLOTS)
    for j in range(2):
        from_head(5, j, dq_blk, dq_mid)

    def sum_up(got, total, n, out):
        wait_all(got, back_recv.at[n])
        acc = jnp.zeros((BLOCKS * ROWS, HEAD_DIM), F32)
        terms = got[...].reshape(PLACES * SLOTS * ROWS, HEAD_DIM)
        wide = jnp.concatenate([spread[k] for k in range(PLACES * SLOTS // 8)], axis=1)
        acc = dot(wide, terms, NN)
        total[...] = acc.astype(BF16).reshape(BLOCKS, ROWS, HEAD_DIM)
        dst = out.at[
            pl.ds(pl.multiple_of(y * ROWS, ROWS), ROWS),
            pl.ds(pl.multiple_of(head * HEAD_DIM, HEAD_DIM), HEAD_DIM),
        ]

        def step(o, _):
            t = lax.rem(ctx + o, BLOCKS)
            pltpu.make_async_remote_copy(
                src_ref=total.at[t],
                dst_ref=dst,
                send_sem=sum_send.at[n],
                recv_sem=sum_recv.at[n],
                device_id=(t, x),
                device_id_type=MESH,
            ).start()
            return 0

        lax.fori_loop(1, BLOCKS, step, 0)
        pltpu.make_async_copy(total.at[ctx], dst, sum_recv.at[n]).start()

    sum_up(dv_got, dv_sum, 0, dv_out)
    wait_all(o_mid, head_recv.at[4])
    each(0, PLACES, lambda e: from_place(6, turned(e), o_mid, o_out))
    wait_all(dq_mid, head_recv.at[5])
    each(0, PLACES, lambda e: from_place(7, turned(e), dq_mid, dq_out))
    sum_up(dk_got, dk_sum, 1, dk_out)

    for n, ref in ((0, k_stripes), (1, v_stripes)):
        wait_all(ref.at[pl.ds(0, BLOCKS - 1)], stripe_send.at[n])
    for n, ref in ((0, k_send), (1, v_send)):
        wait_all(ref.at[pl.ds(0, PLACES - 1)], pick_send.at[n])
    for n, ref in ((0, dv_send), (1, dk_send)):
        wait_all(ref.at[pl.ds(0, PLACES - 1)], back_send.at[n])
    for n, src, mid, dst in ((0, q_in, q_mid, q_blk), (1, g_in, g_mid, g_blk)):
        each(0, PLACES, lambda e: to_place(n, e, src, mid, False))
        each(0, 2, lambda j: to_head(n + 2, j, mid, dst, False))
    for n, src, mid, out in ((4, o_blk, o_mid, o_out), (5, dq_blk, dq_mid, dq_out)):
        each(0, 2, lambda j: from_head(n, j, src, mid, False))
        each(0, PLACES, lambda e: from_place(n + 2, e, mid, out, False))
        wait_all(out, head_recv.at[n + 2])
    for n, ref, out in ((0, dv_sum, dv_out), (1, dk_sum, dk_out)):
        wait_all(ref.at[pl.ds(0, BLOCKS - 1)], sum_send.at[n])
        wait_all(out, sum_recv.at[n])


def hand_over(*refs):
    copies = [pltpu.make_async_copy(refs[n], refs[n + 4], refs[8].at[n]) for n in range(4)]
    for copy in copies:
        copy.start()
    for copy in copies:
        copy.wait()


def per_device(queries, key_rows, value_rows, grad_output, chosen_blocks):
    vmem = pl.BlockSpec(memory_space=pltpu.VMEM)
    shape = jax.ShapeDtypeStruct(queries.shape, BF16)
    dma = pltpu.SemaphoreType.DMA
    stripes = pltpu.VMEM((BLOCKS, ROWS, HEAD_DIM), BF16)
    picks = pltpu.VMEM((PLACES, SLOTS, ROWS, HEAD_DIM), BF16)
    rows = pltpu.VMEM((GROUP * BLOCK, HEAD_DIM), BF16)
    landed = pl.pallas_call(
        kernel,
        out_shape=(shape,) * 4,
        in_specs=[pl.BlockSpec(memory_space=pl.ANY)] * 4 + [pl.BlockSpec(memory_space=pltpu.SMEM)],
        out_specs=(pl.BlockSpec(memory_space=pl.ANY),) * 4,
        scratch_shapes=[
            stripes, stripes, picks, picks, picks, picks, rows, rows, rows, rows,
            pltpu.VMEM((GROUP, 4, BLOCK, BLOCK), BF16),
            rows, rows, rows, rows, picks, picks, picks, picks,
            pltpu.VMEM((PLACES * SLOTS // 8, BLOCKS * ROWS, 128), BF16),
            stripes, stripes,
            pltpu.VMEM((2, BLOCK, HEAD_DIM), F32),
            pltpu.VMEM((GROUP, 1, BLOCK), F32),
            pltpu.SMEM((PLACES * SLOTS,), jnp.int32),
            dma((2,)), dma((2,)), dma((2,)), dma((2,)), dma((8, PLACES)), dma((8,)),
            dma((2,)), dma((2,)), dma((2,)), dma((2,)), dma((2,)), dma((2,)),
        ],
        compiler_params=pltpu.CompilerParams(
            collective_id=0, has_side_effects=True, vmem_limit_bytes=56 * 2**20
        ),
    )(queries, key_rows, value_rows, grad_output, chosen_blocks)
    return pl.pallas_call(
        hand_over,
        out_shape=(shape,) * 4,
        in_specs=[vmem] * 4,
        out_specs=(pl.BlockSpec(memory_space=pl.ANY),) * 4,
        scratch_shapes=[dma((4,))],
    )(*landed)


def solution(mesh):
    placed = P(("ctx", "head"), None)
    return jax.shard_map(
        per_device,
        mesh=mesh,
        in_specs=(placed,) * 4 + (P(),),
        out_specs=(placed,) * 4,
        check_vma=False,
    )
```

```python
import functools

import jax
import jax.numpy as jnp
from jax import lax
from jax.experimental import pallas as pl
from jax.experimental.pallas import tpu as pltpu
from jax.sharding import PartitionSpec as P

MESH = pl.DeviceIdType.MESH
HEAD_DIM = 128
BLOCKS = 64
GROUP = 4
EARLY = 6
SLOTS = 13
PLACES = 16
ROWS = 16
BLOCK = 256
SCALE = HEAD_DIM**-0.5
LOG2E = 1.4426950408889634
BF16 = jnp.bfloat16
F32 = jnp.float32

NT = (((1,), (1,)), ((), ()))
NN = (((1,), (0,)), ((), ()))
TN = (((0,), (0,)), ((), ()))


def dot(a, b, dims):
    return lax.dot_general(a, b, dims, preferred_element_type=F32)


def kernel(
    q_in, k_in, v_in, g_in, chosen,
    o_out, dq_out, dk_out, dv_out,
    k_stripes, v_stripes, k_send, v_send, k_got, v_got, q_mid, g_mid, q_blk, g_blk, probs,
    o_blk, dq_blk, o_mid, dq_mid, dk_send, dv_send, dk_got, dv_got, spread_early, spread_late, early_sum, dk_sum, dv_sum, carry, row_dots, table,
    stripe_send, stripe_recv, pick_send, pick_recv, head_send, head_recv,
    back_send, back_recv, sum_send, sum_recv,
):
    ctx = lax.axis_index("ctx")
    x = lax.axis_index("head")
    z = lax.div(ctx, 8)
    y = lax.rem(lax.div(ctx, 2), 4)
    c = lax.rem(ctx, 2)
    head = 2 * z + c
    place = 4 * x + y

    def group_at(px, py):
        odd, px_low, py_low = lax.div(px, 2), lax.rem(px, 2), lax.rem(py, 2)
        low = (1 - odd) * px_low + odd * lax.rem(py_low + z, 2)
        high = (1 - odd) * lax.rem(py_low + c, 2) + odd * lax.rem(px_low + c, 2)
        return 2 * lax.rem(z + 4 * high + 2 * low + odd, 8) + lax.div(py, 2)

    def place_of(g, e_z, e_c):
        offset = lax.rem(lax.div(g, 2) + 8 - e_z, 8)
        odd, d = lax.rem(offset, 2), lax.div(offset, 2)
        high = lax.rem(lax.div(d, 2) + e_c, 2)
        even_place = 2 * lax.rem(d, 2) + high
        odd_place = 4 + 2 * high + lax.rem(d + e_z, 2)
        t = (1 - odd) * even_place + odd * odd_place
        return lax.div(t, 2), 2 * lax.rem(g, 2) + lax.rem(t, 2)

    group = group_at(x, y)

    def head_z(e_c):
        odd, px_low, py_low = lax.div(x, 2), lax.rem(x, 2), lax.rem(y, 2)
        low = (1 - odd) * px_low + odd * lax.rem(py_low + z + 1, 2)
        high = (1 - odd) * lax.rem(py_low + e_c, 2) + odd * lax.rem(px_low + e_c, 2)
        return lax.rem(z + 8 - (4 * high + 2 * low + odd), 8)

    barrier = pltpu.get_barrier_semaphore()

    def greet(o, _):
        pl.semaphore_signal(
            barrier, inc=1, device_id=(lax.rem(ctx + o, BLOCKS), x), device_id_type=MESH
        )
        return 0

    lax.fori_loop(1, BLOCKS, greet, 0)

    def place_id(p):
        return (8 * z + 2 * lax.rem(p, 4) + c, lax.div(p, 4))

    def greet_place(o, _):
        p = lax.rem(place + o, PLACES)

        @pl.when(lax.div(p, 4) != x)
        def _():
            pl.semaphore_signal(barrier, inc=1, device_id=place_id(p), device_id_type=MESH)

        return 0

    lax.fori_loop(1, PLACES, greet_place, 0)
    pl.semaphore_wait(barrier, BLOCKS - 1 + 12)

    def each(lo, hi, fn):
        def step(e, _):
            fn(e)
            return 0

        lax.fori_loop(lo, hi, step, 0)

    def stripe_src(ref, t):
        t_y = lax.rem(lax.div(t, 2), 4)
        t_head = 2 * lax.div(t, 8) + lax.rem(t, 2)
        return ref.at[
            pl.ds(pl.multiple_of(t_y * ROWS, ROWS), ROWS),
            pl.ds(pl.multiple_of(t_head * HEAD_DIM, HEAD_DIM), HEAD_DIM),
        ]

    def send_stripes(src, dst, n, beside):
        def stripe(o):
            t = lax.rem(ctx + o, BLOCKS)
            pltpu.make_async_remote_copy(
                src_ref=stripe_src(src, t),
                dst_ref=dst.at[ctx],
                send_sem=stripe_send.at[n],
                recv_sem=stripe_recv.at[n],
                device_id=(t, x),
                device_id_type=MESH,
            ).start()

        def step(e, _):
            for o in range(4):
                stripe(4 * e + o)
            beside(e)
            return 0

        for o in range(1, 4):
            stripe(o)
        beside(0)
        lax.fori_loop(1, PLACES, step, 0)
        pltpu.make_async_copy(stripe_src(src, ctx), dst.at[ctx], stripe_recv.at[n]).start()

    def wait_all(ref, sem):
        pltpu.make_async_copy(ref, ref, sem).wait()

    def turned(o):
        return lax.rem(head + o, PLACES)

    def one(n, k, s, d, t, here, mode=True):
        def remote():
            return pltpu.make_async_remote_copy(
                src_ref=s, dst_ref=d, send_sem=head_send.at[n, k], recv_sem=head_recv.at[n],
                device_id=t, device_id_type=MESH,
            )

        @pl.when(jnp.logical_not(here))
        def _():
            if mode:
                remote().start()
            else:
                remote().wait_send()

        if mode:

            @pl.when(here)
            def _():
                pltpu.make_async_copy(s, d, head_recv.at[n]).start()

    def columns(e):
        return pl.ds(pl.multiple_of(e * HEAD_DIM, HEAD_DIM), HEAD_DIM)

    def to_place(n, e, src, mid):
        t_x, t_y = place_of(lax.div(ctx, 4), lax.div(e, 2), lax.rem(e, 2))
        here = jnp.logical_and(t_x == x, t_y == y)
        start = (2 * lax.rem(e, 2) + lax.rem(y, 2)) * BLOCK + x * 64
        one(
            n, 0, src.at[:, columns(e)], mid.at[pl.ds(pl.multiple_of(start, 64), 64), :],
            (8 * z + 2 * t_y + c, t_x), here,
        )

    def half_of(ref, j):
        return ref.at[pl.ds(pl.multiple_of(j * 2 * BLOCK, 2 * BLOCK), 2 * BLOCK), :]

    def to_head(n, j, mid, dst, mode=True):
        e_z = head_z(j)
        here = jnp.logical_and(e_z == z, c == j)
        one(n, j, half_of(mid, j), half_of(dst, c), (8 * e_z + 2 * y + j, x), here, mode)

    def from_head(n, j, src, mid, mode=True):
        t_z = lax.div(group, 2)
        here = jnp.logical_and(t_z == z, c == j)
        one(n, j, half_of(src, j), half_of(mid, c), (8 * t_z + 2 * y + j, x), here, mode)

    def from_place(n, e, mid, out):
        j, low, t_x = lax.div(e, 8), lax.rem(lax.div(e, 4), 2), lax.rem(e, 4)
        t_y = 2 * lax.div(y, 2) + low
        here = jnp.logical_and(t_x == x, t_y == y)
        start = (2 * j + low) * BLOCK + t_x * 64
        one(
            n, 0, mid.at[pl.ds(pl.multiple_of(start, 64), 64), :],
            out.at[:, columns(2 * head_z(j) + j)], (8 * z + 2 * t_y + c, t_x), here,
        )

    def places_sent(n, mid):
        wait_all(mid.at[pl.ds(0, 14 * 64)], head_send.at[n, 0])

    send_stripes(k_in, k_stripes, 0, lambda e: None)
    each(0, PLACES, lambda e: to_place(0, turned(e), q_in, q_mid))
    send_stripes(v_in, v_stripes, 1, lambda e: None)
    each(0, PLACES, lambda e: to_place(1, turned(e), g_in, g_mid))

    def fill_table(p, _):
        g = group_at(lax.div(p, 4), lax.rem(p, 4))
        base = p * SLOTS
        for i in range(GROUP):
            b = 4 * g + i
            e0, e1, e2 = chosen[0, b], chosen[1, b], chosen[2, b]
            table[base + 3 * i] = b - 1
            table[base + 3 * i + 1] = jnp.where(e0 == b - 1, e1, e0)
            table[base + 3 * i + 2] = jnp.where(e2 == b - 1, e1, e2)
        table[base + 12] = 4 * g + 3
        return 0

    lax.fori_loop(0, PLACES, fill_table, 0)

    def send_picks(stripes, out, got, n, beside):
        def step(o, _):
            p = lax.rem(place + o, PLACES)
            for s in range(SLOTS):
                out[p, s] = stripes[jnp.maximum(table[p * SLOTS + s], 0)]
            pltpu.make_async_remote_copy(
                src_ref=out.at[p],
                dst_ref=got.at[place],
                send_sem=pick_send.at[n],
                recv_sem=pick_recv.at[n],
                device_id=place_id(p),
                device_id_type=MESH,
            ).start()
            return 0

        lax.fori_loop(1, 5, step, 0)
        beside()
        lax.fori_loop(5, PLACES, step, 0)
        for s in range(SLOTS):
            got[place, s] = stripes[jnp.maximum(table[place * SLOTS + s], 0)]

    wait_all(k_stripes, stripe_recv.at[0])
    def head_part(n, mid, dst):
        wait_all(mid, head_recv.at[n])
        for j in range(2):
            to_head(n + 2, j, mid, dst)

    send_picks(k_stripes, k_send, k_got, 0, lambda: head_part(0, q_mid, q_blk))
    head_part(1, g_mid, g_blk)
    wait_all(v_stripes, stripe_recv.at[1])
    send_picks(v_stripes, v_send, v_got, 1, lambda: None)

    def block_of(ref, s):
        return ref[:, s].reshape(BLOCK, HEAD_DIM)

    def rows_of(i):
        at = 2 * lax.rem(i, 2) + lax.div(i, 2)
        return pl.ds(pl.multiple_of(at * BLOCK, BLOCK), BLOCK)

    wait_all(q_blk, head_recv.at[2])
    wait_all(k_got.at[pl.ds(0, PLACES - 1)], pick_recv.at[0])

    def soft(i):
        qi = q_blk[rows_of(i), :]
        b = 4 * group + i
        d0 = table[place * SLOTS + 3 * i + 1]
        d1 = table[place * SLOTS + 3 * i + 2]
        keys = lax.broadcasted_iota(jnp.int32, (BLOCK, BLOCK), 0)
        asks = lax.broadcasted_iota(jnp.int32, (BLOCK, BLOCK), 1)
        scores = []
        for s in range(4):
            raw = dot(block_of(k_got, 3 * i + s), qi, NT)
            if s == 3:
                raw = jnp.where(keys <= asks, raw, -jnp.inf)
            else:
                usable = (b, d0 + 1, d1 + 1)[s] > 0
                raw = raw + jnp.where(usable, 0.0, -jnp.inf).astype(F32)
            scores.append(raw)
        peak = functools.reduce(
            jnp.maximum, [jnp.max(r, axis=0, keepdims=True) for r in scores]
        )
        powers = [jnp.exp2((r - peak) * (SCALE * LOG2E)) for r in scores]
        total = functools.reduce(
            jnp.add, [jnp.sum(r, axis=0, keepdims=True) for r in powers]
        )
        inverse = 1.0 / total
        for s in range(4):
            probs[i, s] = (powers[s] * inverse).astype(BF16)

    each(0, GROUP, soft)

    def put(ref, s, value):
        ref[:, s] = value.astype(BF16).reshape(PLACES, ROWS, HEAD_DIM)

    def send_back(src, dst, n, lo, hi):
        def step(o, _):
            p = lax.rem(place + o, PLACES)
            pltpu.make_async_remote_copy(
                src_ref=src.at[p, pl.ds(lo, hi - lo)],
                dst_ref=dst.at[place, pl.ds(lo, hi - lo)],
                send_sem=back_send.at[n],
                recv_sem=back_recv.at[2 * n + (1 if lo else 0)],
                device_id=place_id(p),
                device_id_type=MESH,
            ).start()
            return 0

        lax.fori_loop(1, PLACES, step, 0)
        pltpu.make_async_copy(
            src.at[place, pl.ds(lo, hi - lo)], dst.at[place, pl.ds(lo, hi - lo)],
            back_recv.at[2 * n + (1 if lo else 0)],
        ).start()

    wait_all(g_blk, head_recv.at[3])
    carry[...] = jnp.zeros_like(carry)

    def value_grads(i):
        gi = g_blk[rows_of(i), :]
        for s in range(4):
            dv = dot(probs[i, s], gi, NN)
            if s == 0:
                put(dv_send, 3 * i, dv + carry[0])
            elif s < 3:
                put(dv_send, 3 * i + s, dv)
            else:
                carry[0] = dv

    each(0, 2, value_grads)
    send_back(dv_send, dv_got, 0, 0, EARLY)
    each(2, GROUP, value_grads)
    put(dv_send, SLOTS - 1, carry[0])
    send_back(dv_send, dv_got, 0, EARLY, SLOTS)

    wait_all(v_got.at[pl.ds(0, PLACES - 1)], pick_recv.at[1])

    def outputs(i):
        ot = functools.reduce(
            jnp.add, [dot(block_of(v_got, 3 * i + s), probs[i, s], TN) for s in range(4)]
        )
        out = ot.astype(BF16).astype(F32)
        o_blk[rows_of(i), :] = out.T.astype(BF16)
        row_dots[i] = jnp.sum(g_blk[rows_of(i), :].astype(F32).T * out, axis=0, keepdims=True)

    def score_grads(i):
        qi = q_blk[rows_of(i), :]
        gi = g_blk[rows_of(i), :]
        row_dot = row_dots[i]
        dqt = jnp.zeros((HEAD_DIM, BLOCK), F32)
        for s in range(4):
            dp = dot(block_of(v_got, 3 * i + s), gi, NT)
            ds = (probs[i, s].astype(F32) * (dp - row_dot)).astype(BF16)
            dqt = dqt + dot(block_of(k_got, 3 * i + s), ds, TN)
            dk = dot(ds, qi, NN) * SCALE
            if s == 0:
                put(dk_send, 3 * i, dk + carry[1])
            elif s < 3:
                put(dk_send, 3 * i + s, dk)
            else:
                carry[1] = dk
        dq_blk[rows_of(i), :] = (dqt * SCALE).T.astype(BF16)

    each(0, GROUP, outputs)
    for j in range(2):
        from_head(4, j, o_blk, o_mid)
    each(0, 2, score_grads)
    send_back(dk_send, dk_got, 1, 0, EARLY)
    each(2, GROUP, score_grads)
    put(dk_send, SLOTS - 1, carry[1])
    send_back(dk_send, dk_got, 1, EARLY, SLOTS)
    for j in range(2):
        from_head(5, j, dq_blk, dq_mid)

    lanes = lax.broadcasted_iota(jnp.int32, (1, 128), 1)

    def spread_part(matrix, first, width):
        def chunk(k):
            target = jnp.full((1, 128), -1, jnp.int32)
            for j in range(8):
                pair = 8 * k + j
                entry = lax.div(pair, width) * SLOTS + first + lax.rem(pair, width)
                target = jnp.where(lax.div(lanes, ROWS) == j, table[entry] * ROWS, target)
            target = target + lax.rem(lanes, ROWS)
            rows = lax.broadcasted_iota(jnp.int32, (BLOCKS * ROWS, 128), 0)
            matrix[:, pl.ds(pl.multiple_of(k * 128, 128), 128)] = jnp.where(
                rows == target, 1.0, 0.0
            ).astype(BF16)

        each(0, PLACES * width // 8, chunk)

    spread_part(spread_early, 0, EARLY)
    spread_part(spread_late, EARLY, SLOTS - EARLY)

    def terms(got, lo, hi):
        return got[:, lo:hi].reshape(PLACES * (hi - lo) * ROWS, HEAD_DIM)

    def sum_early(got, n):
        wait_all(got.at[:, pl.ds(0, EARLY)], back_recv.at[2 * n])
        early_sum[...] = dot(spread_early[...], terms(got, 0, EARLY), NN)

    def sum_late(got, total, n, out):
        dst = out.at[
            pl.ds(pl.multiple_of(y * ROWS, ROWS), ROWS),
            pl.ds(pl.multiple_of(head * HEAD_DIM, HEAD_DIM), HEAD_DIM),
        ]

        def quarter(o):
            q = lax.rem(lax.div(ctx, PLACES) + o, 4)
            part = pl.ds(pl.multiple_of(q * BLOCK, BLOCK), BLOCK)
            acc = dot(spread_late[part, :], terms(got, EARLY, SLOTS), NN) + early_sum[part, :]
            total[pl.ds(q * PLACES, PLACES)] = acc.astype(BF16).reshape(PLACES, ROWS, HEAD_DIM)

            def step(k, _):
                t = q * PLACES + lax.rem(ctx + k, PLACES)

                @pl.when(t != ctx)
                def _():
                    pltpu.make_async_remote_copy(
                        src_ref=total.at[t],
                        dst_ref=dst,
                        send_sem=sum_send.at[n],
                        recv_sem=sum_recv.at[n],
                        device_id=(t, x),
                        device_id_type=MESH,
                    ).start()

                return 0

            lax.fori_loop(0, PLACES, step, 0)

        each(0, 4, quarter)
        pltpu.make_async_copy(total.at[ctx], dst, sum_recv.at[n]).start()

    sum_early(dv_got, 0)
    wait_all(dv_got.at[:, pl.ds(EARLY, SLOTS - EARLY)], back_recv.at[1])
    sum_late(dv_got, dv_sum, 0, dv_out)
    sum_early(dk_got, 1)
    for n, ref in ((0, k_stripes), (1, v_stripes)):
        wait_all(ref.at[pl.ds(0, BLOCKS - 1)], stripe_send.at[n])
    for n, ref in ((0, k_send), (1, v_send)):
        wait_all(ref.at[pl.ds(0, PLACES - 1)], pick_send.at[n])
    for n, ref in ((0, dv_send), (1, dk_send)):
        wait_all(ref.at[pl.ds(0, PLACES - 1)], back_send.at[n])
    for n, mid, dst in ((0, q_mid, q_blk), (1, g_mid, g_blk)):
        places_sent(n, mid)
        for j in range(2):
            to_head(n + 2, j, mid, dst, False)
    for n, src, mid in ((4, o_blk, o_mid), (5, dq_blk, dq_mid)):
        for j in range(2):
            from_head(n, j, src, mid, False)
    wait_all(o_mid, head_recv.at[4])
    wait_all(dq_mid, head_recv.at[5])
    wait_all(dk_got.at[:, pl.ds(EARLY, SLOTS - EARLY)], back_recv.at[3])
    each(0, PLACES, lambda e: from_place(6, turned(e), o_mid, o_out))
    each(0, PLACES, lambda e: from_place(7, turned(e), dq_mid, dq_out))
    sum_late(dk_got, dk_sum, 1, dk_out)

    for n, mid, out in ((6, o_mid, o_out), (7, dq_mid, dq_out)):
        places_sent(n, mid)
        wait_all(out, head_recv.at[n])
    for n, ref, out in ((0, dv_sum, dv_out), (1, dk_sum, dk_out)):
        wait_all(ref.at[pl.ds(0, BLOCKS - 1)], sum_send.at[n])
        wait_all(out, sum_recv.at[n])


def hand_over(*refs):
    copies = [pltpu.make_async_copy(refs[n], refs[n + 4], refs[8].at[n]) for n in range(4)]
    for copy in copies:
        copy.start()
    for copy in copies:
        copy.wait()


def per_device(queries, key_rows, value_rows, grad_output, chosen_blocks):
    vmem = pl.BlockSpec(memory_space=pltpu.VMEM)
    shape = jax.ShapeDtypeStruct(queries.shape, BF16)
    dma = pltpu.SemaphoreType.DMA
    stripes = pltpu.VMEM((BLOCKS, ROWS, HEAD_DIM), BF16)
    picks = pltpu.VMEM((PLACES, SLOTS, ROWS, HEAD_DIM), BF16)
    rows = pltpu.VMEM((GROUP * BLOCK, HEAD_DIM), BF16)
    landed = pl.pallas_call(
        kernel,
        out_shape=(shape,) * 4,
        in_specs=[pl.BlockSpec(memory_space=pl.ANY)] * 4 + [pl.BlockSpec(memory_space=pltpu.SMEM)],
        out_specs=(pl.BlockSpec(memory_space=pl.ANY),) * 4,
        scratch_shapes=[
            stripes, stripes, picks, picks, picks, picks, rows, rows, rows, rows,
            pltpu.VMEM((GROUP, 4, BLOCK, BLOCK), BF16),
            rows, rows, rows, rows, picks, picks, picks, picks,
            pltpu.VMEM((BLOCKS * ROWS, PLACES * EARLY * ROWS), BF16),
            pltpu.VMEM((BLOCKS * ROWS, PLACES * (SLOTS - EARLY) * ROWS), BF16),
            pltpu.VMEM((BLOCKS * ROWS, HEAD_DIM), F32),
            stripes, stripes,
            pltpu.VMEM((2, BLOCK, HEAD_DIM), F32),
            pltpu.VMEM((GROUP, 1, BLOCK), F32),
            pltpu.SMEM((PLACES * SLOTS,), jnp.int32),
            dma((2,)), dma((2,)), dma((2,)), dma((2,)), dma((8, 2)), dma((8,)),
            dma((2,)), dma((4,)), dma((2,)), dma((2,)),
        ],
        compiler_params=pltpu.CompilerParams(
            collective_id=0, has_side_effects=True, vmem_limit_bytes=56 * 2**20
        ),
    )(queries, key_rows, value_rows, grad_output, chosen_blocks.T)
    return pl.pallas_call(
        hand_over,
        out_shape=(shape,) * 4,
        in_specs=[vmem] * 4,
        out_specs=(pl.BlockSpec(memory_space=pl.ANY),) * 4,
        scratch_shapes=[dma((4,))],
    )(*landed)


def solution(mesh):
    placed = P(("ctx", "head"), None)
    return jax.shard_map(
        per_device,
        mesh=mesh,
        in_specs=(placed,) * 4 + (P(),),
        out_specs=(placed,) * 4,
        check_vma=False,
    )
```

```python
import functools

import jax
import jax.numpy as jnp
from jax import lax
from jax.experimental import pallas as pl
from jax.experimental.pallas import tpu as pltpu
from jax.sharding import PartitionSpec as P

MESH = pl.DeviceIdType.MESH
HEAD_DIM = 128
BLOCKS = 64
GROUP = 4
STRIPE_STEP = 27
PLACE_STEP = 5
EARLY = 6
SLOTS = 13
PLACES = 16
ROWS = 16
BLOCK = 256
SCALE = HEAD_DIM**-0.5
LOG2E = 1.4426950408889634
BF16 = jnp.bfloat16
F32 = jnp.float32

NT = (((1,), (1,)), ((), ()))
NN = (((1,), (0,)), ((), ()))
TN = (((0,), (0,)), ((), ()))


def dot(a, b, dims):
    return lax.dot_general(a, b, dims, preferred_element_type=F32)


def kernel(
    q_in, k_in, v_in, g_in, chosen,
    o_out, dq_out, dk_out, dv_out,
    k_stripes, v_stripes, k_send, v_send, k_got, v_got, q_mid, g_mid, q_blk, g_blk, probs,
    o_blk, dq_blk, o_mid, dq_mid, dk_send, dv_send, dk_got, dv_got, spread_early, spread_late, early_sum, dk_sum, dv_sum, carry, row_dots, table,
    stripe_send, stripe_recv, pick_send, pick_recv, head_send, head_recv,
    back_send, back_recv, sum_send, sum_recv,
):
    ctx = lax.axis_index("ctx")
    x = lax.axis_index("head")
    z = lax.div(ctx, 8)
    y = lax.rem(lax.div(ctx, 2), 4)
    c = lax.rem(ctx, 2)
    head = 2 * z + c
    place = 4 * x + y

    def group_at(px, py):
        odd, px_low, py_low = lax.div(px, 2), lax.rem(px, 2), lax.rem(py, 2)
        low = (1 - odd) * px_low + odd * lax.rem(py_low + z, 2)
        high = (1 - odd) * lax.rem(py_low + c, 2) + odd * lax.rem(px_low + c, 2)
        return 2 * lax.rem(z + 4 * high + 2 * low + odd, 8) + lax.div(py, 2)

    def place_of(g, e_z, e_c):
        offset = lax.rem(lax.div(g, 2) + 8 - e_z, 8)
        odd, d = lax.rem(offset, 2), lax.div(offset, 2)
        high = lax.rem(lax.div(d, 2) + e_c, 2)
        even_place = 2 * lax.rem(d, 2) + high
        odd_place = 4 + 2 * high + lax.rem(d + e_z, 2)
        t = (1 - odd) * even_place + odd * odd_place
        return lax.div(t, 2), 2 * lax.rem(g, 2) + lax.rem(t, 2)

    group = group_at(x, y)

    def head_z(e_c):
        odd, px_low, py_low = lax.div(x, 2), lax.rem(x, 2), lax.rem(y, 2)
        low = (1 - odd) * px_low + odd * lax.rem(py_low + z + 1, 2)
        high = (1 - odd) * lax.rem(py_low + e_c, 2) + odd * lax.rem(px_low + e_c, 2)
        return lax.rem(z + 8 - (4 * high + 2 * low + odd), 8)

    barrier = pltpu.get_barrier_semaphore()

    def greet(o, _):
        pl.semaphore_signal(
            barrier, inc=1, device_id=(lax.rem(ctx + o, BLOCKS), x), device_id_type=MESH
        )
        return 0

    lax.fori_loop(1, BLOCKS, greet, 0)

    def place_id(p):
        return (8 * z + 2 * lax.rem(p, 4) + c, lax.div(p, 4))

    def greet_place(o, _):
        p = lax.rem(place + o, PLACES)

        @pl.when(lax.div(p, 4) != x)
        def _():
            pl.semaphore_signal(barrier, inc=1, device_id=place_id(p), device_id_type=MESH)

        return 0

    lax.fori_loop(1, PLACES, greet_place, 0)
    pl.semaphore_wait(barrier, BLOCKS - 1 + 12)

    def each(lo, hi, fn):
        def step(e, _):
            fn(e)
            return 0

        lax.fori_loop(lo, hi, step, 0)

    def stripe_src(ref, t):
        t_y = lax.rem(lax.div(t, 2), 4)
        t_head = 2 * lax.div(t, 8) + lax.rem(t, 2)
        return ref.at[
            pl.ds(pl.multiple_of(t_y * ROWS, ROWS), ROWS),
            pl.ds(pl.multiple_of(t_head * HEAD_DIM, HEAD_DIM), HEAD_DIM),
        ]

    def send_stripes(src, dst, n, beside):
        def stripe(o):
            t = lax.rem(ctx + STRIPE_STEP * o, BLOCKS)
            pltpu.make_async_remote_copy(
                src_ref=stripe_src(src, t),
                dst_ref=dst.at[ctx],
                send_sem=stripe_send.at[n],
                recv_sem=stripe_recv.at[n],
                device_id=(t, x),
                device_id_type=MESH,
            ).start()

        def step(e, _):
            for o in range(4):
                stripe(4 * e + o)
            beside(e)
            return 0

        for o in range(1, 4):
            stripe(o)
        beside(0)
        lax.fori_loop(1, PLACES, step, 0)
        pltpu.make_async_copy(stripe_src(src, ctx), dst.at[ctx], stripe_recv.at[n]).start()

    def wait_all(ref, sem):
        pltpu.make_async_copy(ref, ref, sem).wait()

    def turned(o):
        return lax.rem(head + o, PLACES)

    def one(n, k, s, d, t, here, mode=True):
        def remote():
            return pltpu.make_async_remote_copy(
                src_ref=s, dst_ref=d, send_sem=head_send.at[n, k], recv_sem=head_recv.at[n],
                device_id=t, device_id_type=MESH,
            )

        @pl.when(jnp.logical_not(here))
        def _():
            if mode:
                remote().start()
            else:
                remote().wait_send()

        if mode:

            @pl.when(here)
            def _():
                pltpu.make_async_copy(s, d, head_recv.at[n]).start()

    def columns(e):
        return pl.ds(pl.multiple_of(e * HEAD_DIM, HEAD_DIM), HEAD_DIM)

    def to_place(n, e, src, mid):
        t_x, t_y = place_of(lax.div(ctx, 4), lax.div(e, 2), lax.rem(e, 2))
        here = jnp.logical_and(t_x == x, t_y == y)
        start = (2 * lax.rem(e, 2) + lax.rem(y, 2)) * BLOCK + x * 64
        one(
            n, 0, src.at[:, columns(e)], mid.at[pl.ds(pl.multiple_of(start, 64), 64), :],
            (8 * z + 2 * t_y + c, t_x), here,
        )

    def half_of(ref, j):
        return ref.at[pl.ds(pl.multiple_of(j * 2 * BLOCK, 2 * BLOCK), 2 * BLOCK), :]

    def to_head(n, j, mid, dst, mode=True):
        e_z = head_z(j)
        here = jnp.logical_and(e_z == z, c == j)
        one(n, j, half_of(mid, j), half_of(dst, c), (8 * e_z + 2 * y + j, x), here, mode)

    def block_at(ref, at):
        return ref.at[pl.ds(pl.multiple_of(at * BLOCK, BLOCK), BLOCK), :]

    def from_head(n, j, src, mid, part=None):
        t_z = lax.div(group, 2)
        here = jnp.logical_and(t_z == z, c == j)
        ends = (8 * t_z + 2 * y + j, x), here
        if part is None:
            one(n, j, half_of(src, j), half_of(mid, c), *ends, False)
        else:
            one(n, j, block_at(src, 2 * j + part), block_at(mid, 2 * c + part), *ends)

    def from_place(n, e, mid, out):
        j, low, t_x = lax.div(e, 8), lax.rem(lax.div(e, 4), 2), lax.rem(e, 4)
        t_y = 2 * lax.div(y, 2) + low
        here = jnp.logical_and(t_x == x, t_y == y)
        start = (2 * j + low) * BLOCK + t_x * 64
        one(
            n, 0, mid.at[pl.ds(pl.multiple_of(start, 64), 64), :],
            out.at[:, columns(2 * head_z(j) + j)], (8 * z + 2 * t_y + c, t_x), here,
        )

    def places_sent(n, mid):
        wait_all(mid.at[pl.ds(0, 14 * 64)], head_send.at[n, 0])

    send_stripes(k_in, k_stripes, 0, lambda e: None)
    each(0, PLACES, lambda e: to_place(0, turned(e), q_in, q_mid))
    send_stripes(v_in, v_stripes, 1, lambda e: None)
    each(0, PLACES, lambda e: to_place(1, turned(e), g_in, g_mid))

    def fill_table(p, _):
        g = group_at(lax.div(p, 4), lax.rem(p, 4))
        base = p * SLOTS
        for i in range(GROUP):
            b = 4 * g + i
            e0, e1, e2 = chosen[0, b], chosen[1, b], chosen[2, b]
            table[base + 3 * i] = b - 1
            table[base + 3 * i + 1] = jnp.where(e0 == b - 1, e1, e0)
            table[base + 3 * i + 2] = jnp.where(e2 == b - 1, e1, e2)
        table[base + 12] = 4 * g + 3
        return 0

    lax.fori_loop(0, PLACES, fill_table, 0)

    def send_picks(stripes, out, got, n, beside):
        def step(o, _):
            p = lax.rem(place + PLACE_STEP * o, PLACES)
            for s in range(SLOTS):
                out[p, s] = stripes[jnp.maximum(table[p * SLOTS + s], 0)]
            pltpu.make_async_remote_copy(
                src_ref=out.at[p],
                dst_ref=got.at[place],
                send_sem=pick_send.at[n],
                recv_sem=pick_recv.at[n],
                device_id=place_id(p),
                device_id_type=MESH,
            ).start()
            return 0

        lax.fori_loop(1, 4, step, 0)
        beside(0)
        lax.fori_loop(4, 9, step, 0)
        beside(1)
        lax.fori_loop(9, PLACES, step, 0)
        for s in range(SLOTS):
            got[place, s] = stripes[jnp.maximum(table[place * SLOTS + s], 0)]

    wait_all(k_stripes, stripe_recv.at[0])
    def head_part(n, mid, dst):
        wait_all(mid, head_recv.at[n])
        for j in range(2):
            to_head(n + 2, j, mid, dst)

    exchanged = ((q_mid, q_blk), (g_mid, g_blk))
    send_picks(k_stripes, k_send, k_got, 0, lambda n: head_part(n, *exchanged[n]))
    wait_all(v_stripes, stripe_recv.at[1])
    send_picks(v_stripes, v_send, v_got, 1, lambda n: None)

    def block_of(ref, s):
        return ref[:, s].reshape(BLOCK, HEAD_DIM)

    def rows_of(i):
        at = 2 * lax.rem(i, 2) + lax.div(i, 2)
        return pl.ds(pl.multiple_of(at * BLOCK, BLOCK), BLOCK)

    lanes = lax.broadcasted_iota(jnp.int32, (1, 128), 1)

    def spread_part(matrix, first, width):
        def chunk(k):
            target = jnp.full((1, 128), -1, jnp.int32)
            for j in range(8):
                pair = 8 * k + j
                entry = lax.div(pair, width) * SLOTS + first + lax.rem(pair, width)
                target = jnp.where(lax.div(lanes, ROWS) == j, table[entry] * ROWS, target)
            target = target + lax.rem(lanes, ROWS)
            rows = lax.broadcasted_iota(jnp.int32, (BLOCKS * ROWS, 128), 0)
            matrix[:, pl.ds(pl.multiple_of(k * 128, 128), 128)] = jnp.where(
                rows == target, 1.0, 0.0
            ).astype(BF16)

        each(0, PLACES * width // 8, chunk)

    spread_part(spread_early, 0, EARLY)
    spread_part(spread_late, EARLY, SLOTS - EARLY)

    wait_all(q_blk, head_recv.at[2])
    wait_all(k_got.at[pl.ds(0, PLACES - 1)], pick_recv.at[0])

    def soft(i):
        qi = q_blk[rows_of(i), :]
        b = 4 * group + i
        d0 = table[place * SLOTS + 3 * i + 1]
        d1 = table[place * SLOTS + 3 * i + 2]
        keys = lax.broadcasted_iota(jnp.int32, (BLOCK, BLOCK), 0)
        asks = lax.broadcasted_iota(jnp.int32, (BLOCK, BLOCK), 1)
        scores = []
        for s in range(4):
            raw = dot(block_of(k_got, 3 * i + s), qi, NT)
            if s == 3:
                raw = jnp.where(keys <= asks, raw, -jnp.inf)
            else:
                usable = (b, d0 + 1, d1 + 1)[s] > 0
                raw = raw + jnp.where(usable, 0.0, -jnp.inf).astype(F32)
            scores.append(raw)
        peak = functools.reduce(
            jnp.maximum, [jnp.max(r, axis=0, keepdims=True) for r in scores]
        )
        powers = [jnp.exp2((r - peak) * (SCALE * LOG2E)) for r in scores]
        total = functools.reduce(
            jnp.add, [jnp.sum(r, axis=0, keepdims=True) for r in powers]
        )
        inverse = 1.0 / total
        for s in range(4):
            probs[i, s] = (powers[s] * inverse).astype(BF16)

    each(0, GROUP, soft)

    def put(ref, s, value):
        ref[:, s] = value.astype(BF16).reshape(PLACES, ROWS, HEAD_DIM)

    def send_back(src, dst, n, lo, hi):
        def step(o, _):
            p = lax.rem(place + PLACE_STEP * o, PLACES)
            pltpu.make_async_remote_copy(
                src_ref=src.at[p, pl.ds(lo, hi - lo)],
                dst_ref=dst.at[place, pl.ds(lo, hi - lo)],
                send_sem=back_send.at[n],
                recv_sem=back_recv.at[2 * n + (1 if lo else 0)],
                device_id=place_id(p),
                device_id_type=MESH,
            ).start()
            return 0

        lax.fori_loop(1, PLACES, step, 0)
        pltpu.make_async_copy(
            src.at[place, pl.ds(lo, hi - lo)], dst.at[place, pl.ds(lo, hi - lo)],
            back_recv.at[2 * n + (1 if lo else 0)],
        ).start()

    wait_all(g_blk, head_recv.at[3])
    carry[...] = jnp.zeros_like(carry)

    def value_grads(i):
        gi = g_blk[rows_of(i), :]
        for s in range(4):
            dv = dot(probs[i, s], gi, NN)
            if s == 0:
                put(dv_send, 3 * i, dv + carry[0])
            elif s < 3:
                put(dv_send, 3 * i + s, dv)
            else:
                carry[0] = dv

    each(0, 2, value_grads)
    send_back(dv_send, dv_got, 0, 0, EARLY)
    each(2, GROUP, value_grads)
    put(dv_send, SLOTS - 1, carry[0])
    send_back(dv_send, dv_got, 0, EARLY, SLOTS)

    wait_all(v_got.at[pl.ds(0, PLACES - 1)], pick_recv.at[1])

    def outputs(i):
        ot = functools.reduce(
            jnp.add, [dot(block_of(v_got, 3 * i + s), probs[i, s], TN) for s in range(4)]
        )
        out = ot.astype(BF16).astype(F32)
        o_blk[rows_of(i), :] = out.T.astype(BF16)
        row_dots[i] = jnp.sum(g_blk[rows_of(i), :].astype(F32).T * out, axis=0, keepdims=True)

    def score_grads(i):
        qi = q_blk[rows_of(i), :]
        gi = g_blk[rows_of(i), :]
        row_dot = row_dots[i]
        dqt = jnp.zeros((HEAD_DIM, BLOCK), F32)
        for s in range(4):
            dp = dot(block_of(v_got, 3 * i + s), gi, NT)
            ds = (probs[i, s].astype(F32) * (dp - row_dot)).astype(BF16)
            dqt = dqt + dot(block_of(k_got, 3 * i + s), ds, TN)
            dk = dot(ds, qi, NN) * SCALE
            if s == 0:
                put(dk_send, 3 * i, dk + carry[1])
            elif s < 3:
                put(dk_send, 3 * i + s, dk)
            else:
                carry[1] = dk
        dq_blk[rows_of(i), :] = (dqt * SCALE).T.astype(BF16)

    for part in range(2):
        each(2 * part, 2 * part + 2, outputs)
        for j in range(2):
            from_head(4, j, o_blk, o_mid, part)
    each(0, 2, score_grads)
    for j in range(2):
        from_head(5, j, dq_blk, dq_mid, 0)
    send_back(dk_send, dk_got, 1, 0, EARLY)
    each(2, GROUP, score_grads)
    for j in range(2):
        from_head(5, j, dq_blk, dq_mid, 1)
    put(dk_send, SLOTS - 1, carry[1])
    send_back(dk_send, dk_got, 1, EARLY, SLOTS)

    def terms(got, lo, hi):
        return got[:, lo:hi].reshape(PLACES * (hi - lo) * ROWS, HEAD_DIM)

    def sum_early(got, n):
        wait_all(got.at[:, pl.ds(0, EARLY)], back_recv.at[2 * n])
        early_sum[...] = dot(spread_early[...], terms(got, 0, EARLY), NN)

    def sum_late(got, total, n, out):
        dst = out.at[
            pl.ds(pl.multiple_of(y * ROWS, ROWS), ROWS),
            pl.ds(pl.multiple_of(head * HEAD_DIM, HEAD_DIM), HEAD_DIM),
        ]

        def quarter(o):
            q = lax.rem(lax.div(ctx, PLACES) + o, 4)
            part = pl.ds(pl.multiple_of(q * BLOCK, BLOCK), BLOCK)
            acc = dot(spread_late[part, :], terms(got, EARLY, SLOTS), NN) + early_sum[part, :]
            total[pl.ds(q * PLACES, PLACES)] = acc.astype(BF16).reshape(PLACES, ROWS, HEAD_DIM)

            def step(k, _):
                t = q * PLACES + lax.rem(ctx + k, PLACES)

                @pl.when(t != ctx)
                def _():
                    pltpu.make_async_remote_copy(
                        src_ref=total.at[t],
                        dst_ref=dst,
                        send_sem=sum_send.at[n],
                        recv_sem=sum_recv.at[n],
                        device_id=(t, x),
                        device_id_type=MESH,
                    ).start()

                return 0

            lax.fori_loop(0, PLACES, step, 0)

        each(0, 4, quarter)
        pltpu.make_async_copy(total.at[ctx], dst, sum_recv.at[n]).start()

    sum_early(dv_got, 0)
    wait_all(dv_got.at[:, pl.ds(EARLY, SLOTS - EARLY)], back_recv.at[1])
    sum_late(dv_got, dv_sum, 0, dv_out)
    sum_early(dk_got, 1)
    for n, ref in ((0, k_stripes), (1, v_stripes)):
        wait_all(ref.at[pl.ds(0, BLOCKS - 1)], stripe_send.at[n])
    for n, ref in ((0, k_send), (1, v_send)):
        wait_all(ref.at[pl.ds(0, PLACES - 1)], pick_send.at[n])
    for n, ref in ((0, dv_send), (1, dk_send)):
        wait_all(ref.at[pl.ds(0, PLACES - 1)], back_send.at[n])
    for n, mid, dst in ((0, q_mid, q_blk), (1, g_mid, g_blk)):
        places_sent(n, mid)
        for j in range(2):
            to_head(n + 2, j, mid, dst, False)
    for n, src, mid in ((4, o_blk, o_mid), (5, dq_blk, dq_mid)):
        for j in range(2):
            from_head(n, j, src, mid)
    wait_all(o_mid, head_recv.at[4])
    wait_all(dq_mid, head_recv.at[5])
    wait_all(dk_got.at[:, pl.ds(EARLY, SLOTS - EARLY)], back_recv.at[3])
    each(0, PLACES, lambda e: from_place(6, turned(e), o_mid, o_out))
    each(0, PLACES, lambda e: from_place(7, turned(e), dq_mid, dq_out))
    sum_late(dk_got, dk_sum, 1, dk_out)

    for n, mid, out in ((6, o_mid, o_out), (7, dq_mid, dq_out)):
        places_sent(n, mid)
        wait_all(out, head_recv.at[n])
    for n, ref, out in ((0, dv_sum, dv_out), (1, dk_sum, dk_out)):
        wait_all(ref.at[pl.ds(0, BLOCKS - 1)], sum_send.at[n])
        wait_all(out, sum_recv.at[n])


def hand_over(*refs):
    copies = [pltpu.make_async_copy(refs[n], refs[n + 4], refs[8].at[n]) for n in range(4)]
    for copy in copies:
        copy.start()
    for copy in copies:
        copy.wait()


def per_device(queries, key_rows, value_rows, grad_output, chosen_blocks):
    vmem = pl.BlockSpec(memory_space=pltpu.VMEM)
    shape = jax.ShapeDtypeStruct(queries.shape, BF16)
    dma = pltpu.SemaphoreType.DMA
    stripes = pltpu.VMEM((BLOCKS, ROWS, HEAD_DIM), BF16)
    picks = pltpu.VMEM((PLACES, SLOTS, ROWS, HEAD_DIM), BF16)
    rows = pltpu.VMEM((GROUP * BLOCK, HEAD_DIM), BF16)
    landed = pl.pallas_call(
        kernel,
        out_shape=(shape,) * 4,
        in_specs=[pl.BlockSpec(memory_space=pl.ANY)] * 4 + [pl.BlockSpec(memory_space=pltpu.SMEM)],
        out_specs=(pl.BlockSpec(memory_space=pl.ANY),) * 4,
        scratch_shapes=[
            stripes, stripes, picks, picks, picks, picks, rows, rows, rows, rows,
            pltpu.VMEM((GROUP, 4, BLOCK, BLOCK), BF16),
            rows, rows, rows, rows, picks, picks, picks, picks,
            pltpu.VMEM((BLOCKS * ROWS, PLACES * EARLY * ROWS), BF16),
            pltpu.VMEM((BLOCKS * ROWS, PLACES * (SLOTS - EARLY) * ROWS), BF16),
            pltpu.VMEM((BLOCKS * ROWS, HEAD_DIM), F32),
            stripes, stripes,
            pltpu.VMEM((2, BLOCK, HEAD_DIM), F32),
            pltpu.VMEM((GROUP, 1, BLOCK), F32),
            pltpu.SMEM((PLACES * SLOTS,), jnp.int32),
            dma((2,)), dma((2,)), dma((2,)), dma((2,)), dma((8, 2)), dma((8,)),
            dma((2,)), dma((4,)), dma((2,)), dma((2,)),
        ],
        compiler_params=pltpu.CompilerParams(
            collective_id=0, has_side_effects=True, vmem_limit_bytes=56 * 2**20
        ),
    )(queries, key_rows, value_rows, grad_output, chosen_blocks.T)
    return pl.pallas_call(
        hand_over,
        out_shape=(shape,) * 4,
        in_specs=[vmem] * 4,
        out_specs=(pl.BlockSpec(memory_space=pl.ANY),) * 4,
        scratch_shapes=[dma((4,))],
    )(*landed)


def solution(mesh):
    placed = P(("ctx", "head"), None)
    return jax.shard_map(
        per_device,
        mesh=mesh,
        in_specs=(placed,) * 4 + (P(),),
        out_specs=(placed,) * 4,
        check_vma=False,
    )
```

```python
import functools

import jax
import jax.numpy as jnp
from jax import lax
from jax.experimental import pallas as pl
from jax.experimental.pallas import tpu as pltpu
from jax.sharding import PartitionSpec as P

MESH = pl.DeviceIdType.MESH
HEAD_DIM = 128
BLOCKS = 64
GROUP = 4
STRIPE_STEP = 27
PLACE_STEP = 5
EARLY = 6
SLOTS = 13
PLACES = 16
ROWS = 16
BLOCK = 256
SCALE = HEAD_DIM**-0.5
LOG2E = 1.4426950408889634
BF16 = jnp.bfloat16
F32 = jnp.float32

NT = (((1,), (1,)), ((), ()))
NN = (((1,), (0,)), ((), ()))
TN = (((0,), (0,)), ((), ()))


def dot(a, b, dims):
    return lax.dot_general(a, b, dims, preferred_element_type=F32)


def kernel(
    q_in, k_in, v_in, g_in, chosen,
    o_out, dq_out, dk_out, dv_out,
    k_stripes, v_stripes, k_send, v_send, k_got, v_got, q_mid, g_mid, q_blk, g_blk, probs,
    o_blk, dq_blk, o_mid, dq_mid, dk_send, dv_send, dk_got, dv_got, spread_early, spread_late, early_sum, dk_sum, dv_sum, carry, row_dots, table,
    stripe_send, stripe_recv, pick_send, pick_recv, head_send, head_recv,
    back_send, back_recv, sum_send, sum_recv,
):
    ctx = lax.axis_index("ctx")
    x = lax.axis_index("head")
    z = lax.div(ctx, 8)
    y = lax.rem(lax.div(ctx, 2), 4)
    c = lax.rem(ctx, 2)
    head = 2 * z + c
    place = 4 * x + y

    def group_at(px, py):
        odd, px_low, py_low = lax.div(px, 2), lax.rem(px, 2), lax.rem(py, 2)
        low = (1 - odd) * px_low + odd * lax.rem(py_low + z, 2)
        high = (1 - odd) * lax.rem(py_low + c, 2) + odd * lax.rem(px_low + c, 2)
        return 2 * lax.rem(z + 4 * high + 2 * low + odd, 8) + lax.div(py, 2)

    def place_of(g, e_z, e_c):
        offset = lax.rem(lax.div(g, 2) + 8 - e_z, 8)
        odd, d = lax.rem(offset, 2), lax.div(offset, 2)
        high = lax.rem(lax.div(d, 2) + e_c, 2)
        even_place = 2 * lax.rem(d, 2) + high
        odd_place = 4 + 2 * high + lax.rem(d + e_z, 2)
        t = (1 - odd) * even_place + odd * odd_place
        return lax.div(t, 2), 2 * lax.rem(g, 2) + lax.rem(t, 2)

    group = group_at(x, y)

    def head_z(e_c):
        odd, px_low, py_low = lax.div(x, 2), lax.rem(x, 2), lax.rem(y, 2)
        low = (1 - odd) * px_low + odd * lax.rem(py_low + z + 1, 2)
        high = (1 - odd) * lax.rem(py_low + e_c, 2) + odd * lax.rem(px_low + e_c, 2)
        return lax.rem(z + 8 - (4 * high + 2 * low + odd), 8)

    barrier = pltpu.get_barrier_semaphore()

    def greet(o, _):
        pl.semaphore_signal(
            barrier, inc=1, device_id=(lax.rem(ctx + o, BLOCKS), x), device_id_type=MESH
        )
        return 0

    lax.fori_loop(1, BLOCKS, greet, 0)

    def place_id(p):
        return (8 * z + 2 * lax.rem(p, 4) + c, lax.div(p, 4))

    def greet_place(o, _):
        p = lax.rem(place + o, PLACES)

        @pl.when(lax.div(p, 4) != x)
        def _():
            pl.semaphore_signal(barrier, inc=1, device_id=place_id(p), device_id_type=MESH)

        return 0

    lax.fori_loop(1, PLACES, greet_place, 0)
    pl.semaphore_wait(barrier, BLOCKS - 1 + 12)

    def each(lo, hi, fn):
        def step(e, _):
            fn(e)
            return 0

        lax.fori_loop(lo, hi, step, 0)

    def stripe_src(ref, t):
        t_y = lax.rem(lax.div(t, 2), 4)
        t_head = 2 * lax.div(t, 8) + lax.rem(t, 2)
        return ref.at[
            pl.ds(pl.multiple_of(t_y * ROWS, ROWS), ROWS),
            pl.ds(pl.multiple_of(t_head * HEAD_DIM, HEAD_DIM), HEAD_DIM),
        ]

    def send_stripes(src, dst, n, beside):
        def stripe(o):
            t = lax.rem(ctx + STRIPE_STEP * o, BLOCKS)
            pltpu.make_async_remote_copy(
                src_ref=stripe_src(src, t),
                dst_ref=dst.at[ctx],
                send_sem=stripe_send.at[n],
                recv_sem=stripe_recv.at[n],
                device_id=(t, x),
                device_id_type=MESH,
            ).start()

        def step(e, _):
            for o in range(4):
                stripe(4 * e + o)
            beside(e)
            return 0

        for o in range(1, 4):
            stripe(o)
        beside(0)
        lax.fori_loop(1, PLACES, step, 0)
        pltpu.make_async_copy(stripe_src(src, ctx), dst.at[ctx], stripe_recv.at[n]).start()

    def wait_all(ref, sem):
        pltpu.make_async_copy(ref, ref, sem).wait()

    def turned(o):
        return lax.rem(head + o, PLACES)

    def one(n, k, s, d, t, here, mode=True):
        def remote():
            return pltpu.make_async_remote_copy(
                src_ref=s, dst_ref=d, send_sem=head_send.at[n, k], recv_sem=head_recv.at[n],
                device_id=t, device_id_type=MESH,
            )

        @pl.when(jnp.logical_not(here))
        def _():
            if mode:
                remote().start()
            else:
                remote().wait_send()

        if mode:

            @pl.when(here)
            def _():
                pltpu.make_async_copy(s, d, head_recv.at[n]).start()

    def columns(e):
        return pl.ds(pl.multiple_of(e * HEAD_DIM, HEAD_DIM), HEAD_DIM)

    def to_place(n, e, src, mid):
        t_x, t_y = place_of(lax.div(ctx, 4), lax.div(e, 2), lax.rem(e, 2))
        here = jnp.logical_and(t_x == x, t_y == y)
        start = (2 * lax.rem(e, 2) + lax.rem(y, 2)) * BLOCK + x * 64
        one(
            n, 0, src.at[:, columns(e)], mid.at[pl.ds(pl.multiple_of(start, 64), 64), :],
            (8 * z + 2 * t_y + c, t_x), here,
        )

    def half_of(ref, j):
        return ref.at[pl.ds(pl.multiple_of(j * 2 * BLOCK, 2 * BLOCK), 2 * BLOCK), :]

    def to_head(n, j, mid, dst, mode=True):
        e_z = head_z(j)
        here = jnp.logical_and(e_z == z, c == j)
        one(n, j, half_of(mid, j), half_of(dst, c), (8 * e_z + 2 * y + j, x), here, mode)

    def block_at(ref, at):
        return ref.at[pl.ds(pl.multiple_of(at * BLOCK, BLOCK), BLOCK), :]

    def from_head(n, j, src, mid, part=None):
        t_z = lax.div(group, 2)
        here = jnp.logical_and(t_z == z, c == j)
        ends = (8 * t_z + 2 * y + j, x), here
        if part is None:
            one(n, j, half_of(src, j), half_of(mid, c), *ends, False)
        else:
            one(n, j, block_at(src, 2 * j + part), block_at(mid, 2 * c + part), *ends)

    def from_place(n, e, mid, out):
        j, low, t_x = lax.div(e, 8), lax.rem(lax.div(e, 4), 2), lax.rem(e, 4)
        t_y = 2 * lax.div(y, 2) + low
        here = jnp.logical_and(t_x == x, t_y == y)
        start = (2 * j + low) * BLOCK + t_x * 64
        one(
            n, 0, mid.at[pl.ds(pl.multiple_of(start, 64), 64), :],
            out.at[:, columns(2 * head_z(j) + j)], (8 * z + 2 * t_y + c, t_x), here,
        )

    def places_sent(n, mid):
        wait_all(mid.at[pl.ds(0, 14 * 64)], head_send.at[n, 0])

    send_stripes(k_in, k_stripes, 0, lambda e: None)
    each(0, PLACES, lambda e: to_place(0, turned(e), q_in, q_mid))
    send_stripes(v_in, v_stripes, 1, lambda e: None)
    each(0, PLACES, lambda e: to_place(1, turned(e), g_in, g_mid))

    def fill_table(p, _):
        g = group_at(lax.div(p, 4), lax.rem(p, 4))
        base = p * SLOTS
        for i in range(GROUP):
            b = 4 * g + i
            e0, e1, e2 = chosen[0, b], chosen[1, b], chosen[2, b]
            table[base + 3 * i] = b - 1
            table[base + 3 * i + 1] = jnp.where(e0 == b - 1, e1, e0)
            table[base + 3 * i + 2] = jnp.where(e2 == b - 1, e1, e2)
        table[base + 12] = 4 * g + 3
        return 0

    lax.fori_loop(0, PLACES, fill_table, 0)

    def send_picks(stripes, out, got, n, beside):
        def step(o, _):
            p = lax.rem(place + PLACE_STEP * o, PLACES)
            for s in range(SLOTS):
                out[p, s] = stripes[jnp.maximum(table[p * SLOTS + s], 0)]
            pltpu.make_async_remote_copy(
                src_ref=out.at[p],
                dst_ref=got.at[place],
                send_sem=pick_send.at[n],
                recv_sem=pick_recv.at[n],
                device_id=place_id(p),
                device_id_type=MESH,
            ).start()
            return 0

        lax.fori_loop(1, 5, step, 0)
        beside(0)
        lax.fori_loop(5, 11, step, 0)
        beside(1)
        lax.fori_loop(11, PLACES, step, 0)
        for s in range(SLOTS):
            got[place, s] = stripes[jnp.maximum(table[place * SLOTS + s], 0)]

    wait_all(k_stripes, stripe_recv.at[0])
    def head_part(n, mid, dst):
        wait_all(mid, head_recv.at[n])
        for j in range(2):
            to_head(n + 2, j, mid, dst)

    exchanged = ((q_mid, q_blk), (g_mid, g_blk))
    send_picks(k_stripes, k_send, k_got, 0, lambda n: head_part(n, *exchanged[n]))
    wait_all(v_stripes, stripe_recv.at[1])
    send_picks(v_stripes, v_send, v_got, 1, lambda n: None)

    def block_of(ref, s):
        return ref[:, s].reshape(BLOCK, HEAD_DIM)

    def rows_of(i):
        at = 2 * lax.rem(i, 2) + lax.div(i, 2)
        return pl.ds(pl.multiple_of(at * BLOCK, BLOCK), BLOCK)

    lanes = lax.broadcasted_iota(jnp.int32, (1, 128), 1)

    def spread_part(matrix, first, width):
        def chunk(k):
            target = jnp.full((1, 128), -1, jnp.int32)
            for j in range(8):
                pair = 8 * k + j
                entry = lax.div(pair, width) * SLOTS + first + lax.rem(pair, width)
                target = jnp.where(lax.div(lanes, ROWS) == j, table[entry] * ROWS, target)
            target = target + lax.rem(lanes, ROWS)
            rows = lax.broadcasted_iota(jnp.int32, (BLOCKS * ROWS, 128), 0)
            matrix[:, pl.ds(pl.multiple_of(k * 128, 128), 128)] = jnp.where(
                rows == target, 1.0, 0.0
            ).astype(BF16)

        each(0, PLACES * width // 8, chunk)

    spread_part(spread_early, 0, EARLY)
    spread_part(spread_late, EARLY, SLOTS - EARLY)

    wait_all(q_blk, head_recv.at[2])
    wait_all(k_got.at[pl.ds(0, PLACES - 1)], pick_recv.at[0])

    def soft(i):
        qi = q_blk[rows_of(i), :]
        b = 4 * group + i
        d0 = table[place * SLOTS + 3 * i + 1]
        d1 = table[place * SLOTS + 3 * i + 2]
        keys = lax.broadcasted_iota(jnp.int32, (BLOCK, BLOCK), 0)
        asks = lax.broadcasted_iota(jnp.int32, (BLOCK, BLOCK), 1)
        scores = []
        for s in range(4):
            raw = dot(block_of(k_got, 3 * i + s), qi, NT)
            if s == 3:
                raw = jnp.where(keys <= asks, raw, -jnp.inf)
            else:
                usable = (b, d0 + 1, d1 + 1)[s] > 0
                raw = raw + jnp.where(usable, 0.0, -jnp.inf).astype(F32)
            scores.append(raw)
        peak = functools.reduce(
            jnp.maximum, [jnp.max(r, axis=0, keepdims=True) for r in scores]
        )
        powers = [jnp.exp2((r - peak) * (SCALE * LOG2E)) for r in scores]
        total = functools.reduce(
            jnp.add, [jnp.sum(r, axis=0, keepdims=True) for r in powers]
        )
        inverse = 1.0 / total
        for s in range(4):
            probs[i, s] = (powers[s] * inverse).astype(BF16)

    each(0, GROUP, soft)

    def put(ref, s, value):
        ref[:, s] = value.astype(BF16).reshape(PLACES, ROWS, HEAD_DIM)

    def send_back(src, dst, n, lo, hi):
        def step(o, _):
            p = lax.rem(place + PLACE_STEP * o, PLACES)
            pltpu.make_async_remote_copy(
                src_ref=src.at[p, pl.ds(lo, hi - lo)],
                dst_ref=dst.at[place, pl.ds(lo, hi - lo)],
                send_sem=back_send.at[n],
                recv_sem=back_recv.at[2 * n + (1 if lo else 0)],
                device_id=place_id(p),
                device_id_type=MESH,
            ).start()
            return 0

        lax.fori_loop(1, PLACES, step, 0)
        pltpu.make_async_copy(
            src.at[place, pl.ds(lo, hi - lo)], dst.at[place, pl.ds(lo, hi - lo)],
            back_recv.at[2 * n + (1 if lo else 0)],
        ).start()

    wait_all(g_blk, head_recv.at[3])
    carry[...] = jnp.zeros_like(carry)

    def value_grads(i):
        gi = g_blk[rows_of(i), :]
        for s in range(4):
            dv = dot(probs[i, s], gi, NN)
            if s == 0:
                put(dv_send, 3 * i, dv + carry[0])
            elif s < 3:
                put(dv_send, 3 * i + s, dv)
            else:
                carry[0] = dv

    each(0, 2, value_grads)
    send_back(dv_send, dv_got, 0, 0, EARLY)
    each(2, GROUP, value_grads)
    put(dv_send, SLOTS - 1, carry[0])
    send_back(dv_send, dv_got, 0, EARLY, SLOTS)

    wait_all(v_got.at[pl.ds(0, PLACES - 1)], pick_recv.at[1])

    def outputs(i):
        ot = functools.reduce(
            jnp.add, [dot(block_of(v_got, 3 * i + s), probs[i, s], TN) for s in range(4)]
        )
        out = ot.astype(BF16).astype(F32)
        o_blk[rows_of(i), :] = out.T.astype(BF16)
        row_dots[i] = jnp.sum(g_blk[rows_of(i), :].astype(F32).T * out, axis=0, keepdims=True)

    def score_grads(i):
        qi = q_blk[rows_of(i), :]
        gi = g_blk[rows_of(i), :]
        row_dot = row_dots[i]
        dqt = jnp.zeros((HEAD_DIM, BLOCK), F32)
        for s in range(4):
            dp = dot(block_of(v_got, 3 * i + s), gi, NT)
            ds = (probs[i, s].astype(F32) * (dp - row_dot)).astype(BF16)
            dqt = dqt + dot(block_of(k_got, 3 * i + s), ds, TN)
            dk = dot(ds, qi, NN) * SCALE
            if s == 0:
                put(dk_send, 3 * i, dk + carry[1])
            elif s < 3:
                put(dk_send, 3 * i + s, dk)
            else:
                carry[1] = dk
        dq_blk[rows_of(i), :] = (dqt * SCALE).T.astype(BF16)

    for part in range(2):
        each(2 * part, 2 * part + 2, outputs)
        for j in range(2):
            from_head(4, j, o_blk, o_mid, part)
    each(0, 2, score_grads)
    for j in range(2):
        from_head(5, j, dq_blk, dq_mid, 0)
    send_back(dk_send, dk_got, 1, 0, EARLY)
    each(2, GROUP, score_grads)
    for j in range(2):
        from_head(5, j, dq_blk, dq_mid, 1)
    put(dk_send, SLOTS - 1, carry[1])
    send_back(dk_send, dk_got, 1, EARLY, SLOTS)

    def terms(got, lo, hi):
        return got[:, lo:hi].reshape(PLACES * (hi - lo) * ROWS, HEAD_DIM)

    def sum_early(got, n):
        wait_all(got.at[:, pl.ds(0, EARLY)], back_recv.at[2 * n])
        early_sum[...] = dot(spread_early[...], terms(got, 0, EARLY), NN)

    def sum_late(got, total, n, out):
        dst = out.at[
            pl.ds(pl.multiple_of(y * ROWS, ROWS), ROWS),
            pl.ds(pl.multiple_of(head * HEAD_DIM, HEAD_DIM), HEAD_DIM),
        ]

        def quarter(o):
            q = lax.rem(lax.div(ctx, PLACES) + o, 4)
            part = pl.ds(pl.multiple_of(q * BLOCK, BLOCK), BLOCK)
            acc = dot(spread_late[part, :], terms(got, EARLY, SLOTS), NN) + early_sum[part, :]
            total[pl.ds(q * PLACES, PLACES)] = acc.astype(BF16).reshape(PLACES, ROWS, HEAD_DIM)

            def step(k, _):
                t = q * PLACES + lax.rem(ctx + k, PLACES)

                @pl.when(t != ctx)
                def _():
                    pltpu.make_async_remote_copy(
                        src_ref=total.at[t],
                        dst_ref=dst,
                        send_sem=sum_send.at[n],
                        recv_sem=sum_recv.at[n],
                        device_id=(t, x),
                        device_id_type=MESH,
                    ).start()

                return 0

            lax.fori_loop(0, PLACES, step, 0)

        each(0, 4, quarter)
        pltpu.make_async_copy(total.at[ctx], dst, sum_recv.at[n]).start()

    sum_early(dv_got, 0)
    wait_all(dv_got.at[:, pl.ds(EARLY, SLOTS - EARLY)], back_recv.at[1])
    sum_late(dv_got, dv_sum, 0, dv_out)
    sum_early(dk_got, 1)
    for n, ref in ((0, k_stripes), (1, v_stripes)):
        wait_all(ref.at[pl.ds(0, BLOCKS - 1)], stripe_send.at[n])
    for n, ref in ((0, k_send), (1, v_send)):
        wait_all(ref.at[pl.ds(0, PLACES - 1)], pick_send.at[n])
    for n, ref in ((0, dv_send), (1, dk_send)):
        wait_all(ref.at[pl.ds(0, PLACES - 1)], back_send.at[n])
    for n, mid, dst in ((0, q_mid, q_blk), (1, g_mid, g_blk)):
        places_sent(n, mid)
        for j in range(2):
            to_head(n + 2, j, mid, dst, False)
    for n, src, mid in ((4, o_blk, o_mid), (5, dq_blk, dq_mid)):
        for j in range(2):
            from_head(n, j, src, mid)
    wait_all(o_mid, head_recv.at[4])
    wait_all(dq_mid, head_recv.at[5])
    wait_all(dk_got.at[:, pl.ds(EARLY, SLOTS - EARLY)], back_recv.at[3])
    each(0, PLACES, lambda e: from_place(6, turned(e), o_mid, o_out))
    each(0, PLACES, lambda e: from_place(7, turned(e), dq_mid, dq_out))
    sum_late(dk_got, dk_sum, 1, dk_out)

    for n, mid, out in ((6, o_mid, o_out), (7, dq_mid, dq_out)):
        places_sent(n, mid)
        wait_all(out, head_recv.at[n])
    for n, ref, out in ((0, dv_sum, dv_out), (1, dk_sum, dk_out)):
        wait_all(ref.at[pl.ds(0, BLOCKS - 1)], sum_send.at[n])
        wait_all(out, sum_recv.at[n])


def hand_over(*refs):
    landed, outs, held, sems = refs[:4], refs[4:8], refs[8], refs[9]
    reads = [pltpu.make_async_copy(landed[n], held.at[n], sems.at[0, n]) for n in range(4)]
    writes = [pltpu.make_async_copy(held.at[n], outs[n], sems.at[1, n]) for n in range(4)]
    for read in reads:
        read.start()
    for read, write in zip(reads, writes):
        read.wait()
        write.start()
    for write in writes:
        write.wait()


def per_device(queries, key_rows, value_rows, grad_output, chosen_blocks):
    vmem = pl.BlockSpec(memory_space=pltpu.VMEM)
    shape = jax.ShapeDtypeStruct(queries.shape, BF16)
    dma = pltpu.SemaphoreType.DMA
    stripes = pltpu.VMEM((BLOCKS, ROWS, HEAD_DIM), BF16)
    picks = pltpu.VMEM((PLACES, SLOTS, ROWS, HEAD_DIM), BF16)
    rows = pltpu.VMEM((GROUP * BLOCK, HEAD_DIM), BF16)
    landed = pl.pallas_call(
        kernel,
        out_shape=(shape,) * 4,
        in_specs=[pl.BlockSpec(memory_space=pl.ANY)] * 4 + [pl.BlockSpec(memory_space=pltpu.SMEM)],
        out_specs=(pl.BlockSpec(memory_space=pl.ANY),) * 4,
        scratch_shapes=[
            stripes, stripes, picks, picks, picks, picks, rows, rows, rows, rows,
            pltpu.VMEM((GROUP, 4, BLOCK, BLOCK), BF16),
            rows, rows, rows, rows, picks, picks, picks, picks,
            pltpu.VMEM((BLOCKS * ROWS, PLACES * EARLY * ROWS), BF16),
            pltpu.VMEM((BLOCKS * ROWS, PLACES * (SLOTS - EARLY) * ROWS), BF16),
            pltpu.VMEM((BLOCKS * ROWS, HEAD_DIM), F32),
            stripes, stripes,
            pltpu.VMEM((2, BLOCK, HEAD_DIM), F32),
            pltpu.VMEM((GROUP, 1, BLOCK), F32),
            pltpu.SMEM((PLACES * SLOTS,), jnp.int32),
            dma((2,)), dma((2,)), dma((2,)), dma((2,)), dma((8, 2)), dma((8,)),
            dma((2,)), dma((4,)), dma((2,)), dma((2,)),
        ],
        compiler_params=pltpu.CompilerParams(
            collective_id=0, has_side_effects=True, vmem_limit_bytes=56 * 2**20
        ),
    )(queries, key_rows, value_rows, grad_output, chosen_blocks.T)
    return pl.pallas_call(
        hand_over,
        out_shape=(shape,) * 4,
        in_specs=[pl.BlockSpec(memory_space=pl.ANY)] * 4,
        out_specs=(pl.BlockSpec(memory_space=pl.ANY),) * 4,
        scratch_shapes=[pltpu.VMEM((4,) + queries.shape, BF16), dma((2, 4))],
    )(*landed)


def solution(mesh):
    placed = P(("ctx", "head"), None)
    return jax.shard_map(
        per_device,
        mesh=mesh,
        in_specs=(placed,) * 4 + (P(),),
        out_specs=(placed,) * 4,
        check_vma=False,
    )
```

```python
import functools

import jax
import jax.numpy as jnp
from jax import lax
from jax.experimental import pallas as pl
from jax.experimental.pallas import tpu as pltpu
from jax.sharding import PartitionSpec as P

MESH = pl.DeviceIdType.MESH
HEAD_DIM = 128
BLOCKS = 64
GROUP = 4
STRIPE_STEP = 27
PLACE_STEP = 5
EARLY = 6
SLOTS = 13
PLACES = 16
ROWS = 16
BLOCK = 256
SCALE = HEAD_DIM**-0.5
LOG2E = 1.4426950408889634
BF16 = jnp.bfloat16
F32 = jnp.float32

NT = (((1,), (1,)), ((), ()))
NN = (((1,), (0,)), ((), ()))
TN = (((0,), (0,)), ((), ()))


def dot(a, b, dims):
    return lax.dot_general(a, b, dims, preferred_element_type=F32)


def kernel(
    q_in, k_in, v_in, g_in, chosen,
    o_out, dq_out, dk_out, dv_out,
    k_stripes, v_stripes, k_send, v_send, k_got, v_got, q_mid, g_mid, q_blk, g_blk, probs,
    o_blk, dq_blk, o_mid, dq_mid, dk_send, dv_send, dk_got, dv_got, spread_early, spread_late, early_sum, dk_sum, dv_sum, carry, row_dots, table,
    stripe_send, stripe_recv, pick_send, pick_recv, head_send, head_recv,
    back_send, back_recv, sum_send, sum_recv,
):
    ctx = lax.axis_index("ctx")
    x = lax.axis_index("head")
    z = lax.div(ctx, 8)
    y = lax.rem(lax.div(ctx, 2), 4)
    c = lax.rem(ctx, 2)
    head = 2 * z + c
    place = 4 * x + y

    def group_at(px, py):
        odd, px_low, py_low = lax.div(px, 2), lax.rem(px, 2), lax.rem(py, 2)
        low = (1 - odd) * px_low + odd * lax.rem(py_low + z, 2)
        high = (1 - odd) * lax.rem(py_low + c, 2) + odd * lax.rem(px_low + c, 2)
        return 2 * lax.rem(z + 4 * high + 2 * low + odd, 8) + lax.div(py, 2)

    def place_of(g, e_z, e_c):
        offset = lax.rem(lax.div(g, 2) + 8 - e_z, 8)
        odd, d = lax.rem(offset, 2), lax.div(offset, 2)
        high = lax.rem(lax.div(d, 2) + e_c, 2)
        even_place = 2 * lax.rem(d, 2) + high
        odd_place = 4 + 2 * high + lax.rem(d + e_z, 2)
        t = (1 - odd) * even_place + odd * odd_place
        return lax.div(t, 2), 2 * lax.rem(g, 2) + lax.rem(t, 2)

    group = group_at(x, y)

    def head_z(e_c):
        odd, px_low, py_low = lax.div(x, 2), lax.rem(x, 2), lax.rem(y, 2)
        low = (1 - odd) * px_low + odd * lax.rem(py_low + z + 1, 2)
        high = (1 - odd) * lax.rem(py_low + e_c, 2) + odd * lax.rem(px_low + e_c, 2)
        return lax.rem(z + 8 - (4 * high + 2 * low + odd), 8)

    barrier = pltpu.get_barrier_semaphore()

    def greet(o, _):
        pl.semaphore_signal(
            barrier, inc=1, device_id=(lax.rem(ctx + o, BLOCKS), x), device_id_type=MESH
        )
        return 0

    lax.fori_loop(1, BLOCKS, greet, 0)

    def place_id(p):
        return (8 * z + 2 * lax.rem(p, 4) + c, lax.div(p, 4))

    def greet_place(o, _):
        p = lax.rem(place + o, PLACES)

        @pl.when(lax.div(p, 4) != x)
        def _():
            pl.semaphore_signal(barrier, inc=1, device_id=place_id(p), device_id_type=MESH)

        return 0

    lax.fori_loop(1, PLACES, greet_place, 0)
    pl.semaphore_wait(barrier, BLOCKS - 1 + 12)

    def each(lo, hi, fn):
        def step(e, _):
            fn(e)
            return 0

        lax.fori_loop(lo, hi, step, 0)

    def stripe_src(ref, t):
        t_y = lax.rem(lax.div(t, 2), 4)
        t_head = 2 * lax.div(t, 8) + lax.rem(t, 2)
        return ref.at[
            pl.ds(pl.multiple_of(t_y * ROWS, ROWS), ROWS),
            pl.ds(pl.multiple_of(t_head * HEAD_DIM, HEAD_DIM), HEAD_DIM),
        ]

    def send_stripes(src, dst, n, beside):
        def stripe(o):
            t = lax.rem(ctx + STRIPE_STEP * o, BLOCKS)
            pltpu.make_async_remote_copy(
                src_ref=stripe_src(src, t),
                dst_ref=dst.at[ctx],
                send_sem=stripe_send.at[n],
                recv_sem=stripe_recv.at[n],
                device_id=(t, x),
                device_id_type=MESH,
            ).start()

        def step(e, _):
            for o in range(4):
                stripe(4 * e + o)
            beside(e)
            return 0

        for o in range(1, 4):
            stripe(o)
        beside(0)
        lax.fori_loop(1, PLACES, step, 0)
        pltpu.make_async_copy(stripe_src(src, ctx), dst.at[ctx], stripe_recv.at[n]).start()

    def wait_all(ref, sem):
        pltpu.make_async_copy(ref, ref, sem).wait()

    def turned(o):
        return lax.rem(head + o, PLACES)

    def one(n, k, s, d, t, here, mode=True):
        def remote():
            return pltpu.make_async_remote_copy(
                src_ref=s, dst_ref=d, send_sem=head_send.at[n, k], recv_sem=head_recv.at[n],
                device_id=t, device_id_type=MESH,
            )

        @pl.when(jnp.logical_not(here))
        def _():
            if mode:
                remote().start()
            else:
                remote().wait_send()

        if mode:

            @pl.when(here)
            def _():
                pltpu.make_async_copy(s, d, head_recv.at[n]).start()

    def columns(e):
        return pl.ds(pl.multiple_of(e * HEAD_DIM, HEAD_DIM), HEAD_DIM)

    def to_place(n, e, src, mid):
        t_x, t_y = place_of(lax.div(ctx, 4), lax.div(e, 2), lax.rem(e, 2))
        here = jnp.logical_and(t_x == x, t_y == y)
        start = (2 * lax.rem(e, 2) + lax.rem(y, 2)) * BLOCK + x * 64
        one(
            n, 0, src.at[:, columns(e)], mid.at[pl.ds(pl.multiple_of(start, 64), 64), :],
            (8 * z + 2 * t_y + c, t_x), here,
        )

    def half_of(ref, j):
        return ref.at[pl.ds(pl.multiple_of(j * 2 * BLOCK, 2 * BLOCK), 2 * BLOCK), :]

    def to_head(n, j, mid, dst, mode=True):
        e_z = head_z(j)
        here = jnp.logical_and(e_z == z, c == j)
        one(n, j, half_of(mid, j), half_of(dst, c), (8 * e_z + 2 * y + j, x), here, mode)

    def block_at(ref, at):
        return ref.at[pl.ds(pl.multiple_of(at * BLOCK, BLOCK), BLOCK), :]

    def from_head(n, j, src, mid, part=None):
        t_z = lax.div(group, 2)
        here = jnp.logical_and(t_z == z, c == j)
        ends = (8 * t_z + 2 * y + j, x), here
        if part is None:
            one(n, j, half_of(src, j), half_of(mid, c), *ends, False)
        else:
            one(n, j, block_at(src, 2 * j + part), block_at(mid, 2 * c + part), *ends)

    def from_place(n, e, mid, out):
        j, low, t_x = lax.div(e, 8), lax.rem(lax.div(e, 4), 2), lax.rem(e, 4)
        t_y = 2 * lax.div(y, 2) + low
        here = jnp.logical_and(t_x == x, t_y == y)
        start = (2 * j + low) * BLOCK + t_x * 64
        one(
            n, 0, mid.at[pl.ds(pl.multiple_of(start, 64), 64), :],
            out.at[:, columns(2 * head_z(j) + j)], (8 * z + 2 * t_y + c, t_x), here,
        )

    def places_sent(n, mid):
        wait_all(mid.at[pl.ds(0, 14 * 64)], head_send.at[n, 0])

    send_stripes(k_in, k_stripes, 0, lambda e: None)
    each(0, PLACES, lambda e: to_place(0, turned(e), q_in, q_mid))
    send_stripes(v_in, v_stripes, 1, lambda e: None)
    each(0, PLACES, lambda e: to_place(1, turned(e), g_in, g_mid))

    def fill_table(p, _):
        g = group_at(lax.div(p, 4), lax.rem(p, 4))
        base = p * SLOTS
        for i in range(GROUP):
            b = 4 * g + i
            e0, e1, e2 = chosen[0, b], chosen[1, b], chosen[2, b]
            table[base + 3 * i] = b - 1
            table[base + 3 * i + 1] = jnp.where(e0 == b - 1, e1, e0)
            table[base + 3 * i + 2] = jnp.where(e2 == b - 1, e1, e2)
        table[base + 12] = 4 * g + 3
        return 0

    lax.fori_loop(0, PLACES, fill_table, 0)

    def send_picks(stripes, out, got, n, beside):
        def step(o, _):
            p = lax.rem(place + PLACE_STEP * o, PLACES)
            for s in range(SLOTS):
                out[p, s] = stripes[jnp.maximum(table[p * SLOTS + s], 0)]
            pltpu.make_async_remote_copy(
                src_ref=out.at[p],
                dst_ref=got.at[place],
                send_sem=pick_send.at[n],
                recv_sem=pick_recv.at[n],
                device_id=place_id(p),
                device_id_type=MESH,
            ).start()
            return 0

        lax.fori_loop(1, 5, step, 0)
        beside(0)
        lax.fori_loop(5, 11, step, 0)
        beside(1)
        lax.fori_loop(11, PLACES, step, 0)
        for s in range(SLOTS):
            got[place, s] = stripes[jnp.maximum(table[place * SLOTS + s], 0)]

    wait_all(k_stripes, stripe_recv.at[0])
    def head_part(n, mid, dst):
        wait_all(mid, head_recv.at[n])
        for j in range(2):
            to_head(n + 2, j, mid, dst)

    exchanged = ((q_mid, q_blk), (g_mid, g_blk))
    send_picks(k_stripes, k_send, k_got, 0, lambda n: head_part(n, *exchanged[n]))
    wait_all(v_stripes, stripe_recv.at[1])
    send_picks(v_stripes, v_send, v_got, 1, lambda n: None)

    def block_of(ref, s):
        return ref[:, s].reshape(BLOCK, HEAD_DIM)

    def rows_of(i):
        at = 2 * lax.rem(i, 2) + lax.div(i, 2)
        return pl.ds(pl.multiple_of(at * BLOCK, BLOCK), BLOCK)

    lanes = lax.broadcasted_iota(jnp.int32, (1, 128), 1)

    def spread_part(matrix, first, width):
        def chunk(k):
            target = jnp.full((1, 128), -1, jnp.int32)
            for j in range(8):
                pair = 8 * k + j
                entry = lax.div(pair, width) * SLOTS + first + lax.rem(pair, width)
                target = jnp.where(lax.div(lanes, ROWS) == j, table[entry] * ROWS, target)
            target = target + lax.rem(lanes, ROWS)
            rows = lax.broadcasted_iota(jnp.int32, (BLOCKS * ROWS, 128), 0)
            matrix[:, pl.ds(pl.multiple_of(k * 128, 128), 128)] = jnp.where(
                rows == target, 1.0, 0.0
            ).astype(BF16)

        each(0, PLACES * width // 8, chunk)

    spread_part(spread_early, 0, EARLY)
    spread_part(spread_late, EARLY, SLOTS - EARLY)

    wait_all(q_blk, head_recv.at[2])
    wait_all(k_got.at[pl.ds(0, PLACES - 1)], pick_recv.at[0])

    def soft(i):
        qi = q_blk[rows_of(i), :]
        b = 4 * group + i
        d0 = table[place * SLOTS + 3 * i + 1]
        d1 = table[place * SLOTS + 3 * i + 2]
        keys = lax.broadcasted_iota(jnp.int32, (BLOCK, BLOCK), 0)
        asks = lax.broadcasted_iota(jnp.int32, (BLOCK, BLOCK), 1)
        scores = []
        for s in range(4):
            raw = dot(block_of(k_got, 3 * i + s), qi, NT)
            if s == 3:
                raw = jnp.where(keys <= asks, raw, -jnp.inf)
            else:
                usable = (b, d0 + 1, d1 + 1)[s] > 0
                raw = raw + jnp.where(usable, 0.0, -jnp.inf).astype(F32)
            scores.append(raw)
        peak = functools.reduce(
            jnp.maximum, [jnp.max(r, axis=0, keepdims=True) for r in scores]
        )
        powers = [jnp.exp2((r - peak) * (SCALE * LOG2E)) for r in scores]
        total = functools.reduce(
            jnp.add, [jnp.sum(r, axis=0, keepdims=True) for r in powers]
        )
        inverse = 1.0 / total
        for s in range(4):
            probs[i, s] = (powers[s] * inverse).astype(BF16)

    each(0, GROUP, soft)

    def put(ref, s, value):
        ref[:, s] = value.astype(BF16).reshape(PLACES, ROWS, HEAD_DIM)

    def send_back(src, dst, n, lo, hi):
        def step(o, _):
            p = lax.rem(place + PLACE_STEP * o, PLACES)
            pltpu.make_async_remote_copy(
                src_ref=src.at[p, pl.ds(lo, hi - lo)],
                dst_ref=dst.at[place, pl.ds(lo, hi - lo)],
                send_sem=back_send.at[n],
                recv_sem=back_recv.at[2 * n + (1 if lo else 0)],
                device_id=place_id(p),
                device_id_type=MESH,
            ).start()
            return 0

        lax.fori_loop(1, PLACES, step, 0)
        pltpu.make_async_copy(
            src.at[place, pl.ds(lo, hi - lo)], dst.at[place, pl.ds(lo, hi - lo)],
            back_recv.at[2 * n + (1 if lo else 0)],
        ).start()

    wait_all(g_blk, head_recv.at[3])
    carry[...] = jnp.zeros_like(carry)

    def value_grads(i):
        gi = g_blk[rows_of(i), :]
        for s in range(4):
            dv = dot(probs[i, s], gi, NN)
            if s == 0:
                put(dv_send, 3 * i, dv + carry[0])
            elif s < 3:
                put(dv_send, 3 * i + s, dv)
            else:
                carry[0] = dv

    each(0, 2, value_grads)
    send_back(dv_send, dv_got, 0, 0, EARLY)
    each(2, GROUP, value_grads)
    put(dv_send, SLOTS - 1, carry[0])
    send_back(dv_send, dv_got, 0, EARLY, SLOTS)

    wait_all(v_got.at[pl.ds(0, PLACES - 1)], pick_recv.at[1])

    def outputs(i):
        ot = functools.reduce(
            jnp.add, [dot(block_of(v_got, 3 * i + s), probs[i, s], TN) for s in range(4)]
        )
        out = ot.astype(BF16).astype(F32)
        o_blk[rows_of(i), :] = out.T.astype(BF16)
        row_dots[i] = jnp.sum(g_blk[rows_of(i), :].astype(F32).T * out, axis=0, keepdims=True)

    def score_grads(i):
        qi = q_blk[rows_of(i), :]
        gi = g_blk[rows_of(i), :]
        row_dot = row_dots[i]
        dqt = jnp.zeros((HEAD_DIM, BLOCK), F32)
        for s in range(4):
            dp = dot(block_of(v_got, 3 * i + s), gi, NT)
            ds = (probs[i, s].astype(F32) * (dp - row_dot)).astype(BF16)
            dqt = dqt + dot(block_of(k_got, 3 * i + s), ds, TN)
            dk = dot(ds, qi, NN) * SCALE
            if s == 0:
                put(dk_send, 3 * i, dk + carry[1])
            elif s < 3:
                put(dk_send, 3 * i + s, dk)
            else:
                carry[1] = dk
        dq_blk[rows_of(i), :] = (dqt * SCALE).T.astype(BF16)

    for part in range(2):
        each(2 * part, 2 * part + 2, outputs)
        for j in range(2):
            from_head(4, j, o_blk, o_mid, part)
    each(0, 2, score_grads)
    for j in range(2):
        from_head(5, j, dq_blk, dq_mid, 0)
    send_back(dk_send, dk_got, 1, 0, EARLY)
    each(2, 3, score_grads)
    from_head(5, 0, dq_blk, dq_mid, 1)
    send_back(dk_send, dk_got, 1, EARLY, EARLY + 3)
    each(3, GROUP, score_grads)
    from_head(5, 1, dq_blk, dq_mid, 1)
    put(dk_send, SLOTS - 1, carry[1])
    send_back(dk_send, dk_got, 1, EARLY + 3, SLOTS)

    def terms(got, lo, hi):
        return got[:, lo:hi].reshape(PLACES * (hi - lo) * ROWS, HEAD_DIM)

    def sum_early(got, n):
        wait_all(got.at[:, pl.ds(0, EARLY)], back_recv.at[2 * n])
        early_sum[...] = dot(spread_early[...], terms(got, 0, EARLY), NN)

    def sum_late(got, total, n, out):
        dst = out.at[
            pl.ds(pl.multiple_of(y * ROWS, ROWS), ROWS),
            pl.ds(pl.multiple_of(head * HEAD_DIM, HEAD_DIM), HEAD_DIM),
        ]

        def quarter(o):
            q = lax.rem(lax.div(ctx, PLACES) + o, 4)
            part = pl.ds(pl.multiple_of(q * BLOCK, BLOCK), BLOCK)
            acc = dot(spread_late[part, :], terms(got, EARLY, SLOTS), NN) + early_sum[part, :]
            total[pl.ds(q * PLACES, PLACES)] = acc.astype(BF16).reshape(PLACES, ROWS, HEAD_DIM)

            def step(k, _):
                t = q * PLACES + lax.rem(ctx + k, PLACES)

                @pl.when(t != ctx)
                def _():
                    pltpu.make_async_remote_copy(
                        src_ref=total.at[t],
                        dst_ref=dst,
                        send_sem=sum_send.at[n],
                        recv_sem=sum_recv.at[n],
                        device_id=(t, x),
                        device_id_type=MESH,
                    ).start()

                return 0

            lax.fori_loop(0, PLACES, step, 0)

        each(0, 4, quarter)
        pltpu.make_async_copy(total.at[ctx], dst, sum_recv.at[n]).start()

    sum_early(dv_got, 0)
    wait_all(dv_got.at[:, pl.ds(EARLY, SLOTS - EARLY)], back_recv.at[1])
    sum_late(dv_got, dv_sum, 0, dv_out)
    wait_all(o_mid, head_recv.at[4])
    each(0, PLACES, lambda e: from_place(6, turned(e), o_mid, o_out))
    sum_early(dk_got, 1)
    for n, ref in ((0, k_stripes), (1, v_stripes)):
        wait_all(ref.at[pl.ds(0, BLOCKS - 1)], stripe_send.at[n])
    for n, ref in ((0, k_send), (1, v_send)):
        wait_all(ref.at[pl.ds(0, PLACES - 1)], pick_send.at[n])
    for n, ref in ((0, dv_send), (1, dk_send)):
        wait_all(ref.at[pl.ds(0, PLACES - 1)], back_send.at[n])
    for n, mid, dst in ((0, q_mid, q_blk), (1, g_mid, g_blk)):
        places_sent(n, mid)
        for j in range(2):
            to_head(n + 2, j, mid, dst, False)
    for n, src, mid in ((4, o_blk, o_mid), (5, dq_blk, dq_mid)):
        for j in range(2):
            from_head(n, j, src, mid)
    wait_all(dq_mid, head_recv.at[5])
    wait_all(dk_got.at[:, pl.ds(EARLY, SLOTS - EARLY)], back_recv.at[3])
    each(0, PLACES, lambda e: from_place(7, turned(e), dq_mid, dq_out))
    sum_late(dk_got, dk_sum, 1, dk_out)

    for n, mid, out in ((6, o_mid, o_out), (7, dq_mid, dq_out)):
        places_sent(n, mid)
        wait_all(out, head_recv.at[n])
    for n, ref, out in ((0, dv_sum, dv_out), (1, dk_sum, dk_out)):
        wait_all(ref.at[pl.ds(0, BLOCKS - 1)], sum_send.at[n])
        wait_all(out, sum_recv.at[n])


def hand_over(*refs):
    landed, outs, held, sems = refs[:4], refs[4:8], refs[8], refs[9]
    reads = [pltpu.make_async_copy(landed[n], held.at[n], sems.at[0, n]) for n in range(4)]
    writes = [pltpu.make_async_copy(held.at[n], outs[n], sems.at[1, n]) for n in range(4)]
    for read in reads:
        read.start()
    for read, write in zip(reads, writes):
        read.wait()
        write.start()
    for write in writes:
        write.wait()


def per_device(queries, key_rows, value_rows, grad_output, chosen_blocks):
    vmem = pl.BlockSpec(memory_space=pltpu.VMEM)
    shape = jax.ShapeDtypeStruct(queries.shape, BF16)
    dma = pltpu.SemaphoreType.DMA
    stripes = pltpu.VMEM((BLOCKS, ROWS, HEAD_DIM), BF16)
    picks = pltpu.VMEM((PLACES, SLOTS, ROWS, HEAD_DIM), BF16)
    rows = pltpu.VMEM((GROUP * BLOCK, HEAD_DIM), BF16)
    landed = pl.pallas_call(
        kernel,
        out_shape=(shape,) * 4,
        in_specs=[pl.BlockSpec(memory_space=pl.ANY)] * 4 + [pl.BlockSpec(memory_space=pltpu.SMEM)],
        out_specs=(pl.BlockSpec(memory_space=pl.ANY),) * 4,
        scratch_shapes=[
            stripes, stripes, picks, picks, picks, picks, rows, rows, rows, rows,
            pltpu.VMEM((GROUP, 4, BLOCK, BLOCK), BF16),
            rows, rows, rows, rows, picks, picks, picks, picks,
            pltpu.VMEM((BLOCKS * ROWS, PLACES * EARLY * ROWS), BF16),
            pltpu.VMEM((BLOCKS * ROWS, PLACES * (SLOTS - EARLY) * ROWS), BF16),
            pltpu.VMEM((BLOCKS * ROWS, HEAD_DIM), F32),
            stripes, stripes,
            pltpu.VMEM((2, BLOCK, HEAD_DIM), F32),
            pltpu.VMEM((GROUP, 1, BLOCK), F32),
            pltpu.SMEM((PLACES * SLOTS,), jnp.int32),
            dma((2,)), dma((2,)), dma((2,)), dma((2,)), dma((8, 2)), dma((8,)),
            dma((2,)), dma((4,)), dma((2,)), dma((2,)),
        ],
        compiler_params=pltpu.CompilerParams(
            collective_id=0, has_side_effects=True, vmem_limit_bytes=56 * 2**20
        ),
    )(queries, key_rows, value_rows, grad_output, chosen_blocks.T)
    return pl.pallas_call(
        hand_over,
        out_shape=(shape,) * 4,
        in_specs=[pl.BlockSpec(memory_space=pl.ANY)] * 4,
        out_specs=(pl.BlockSpec(memory_space=pl.ANY),) * 4,
        scratch_shapes=[pltpu.VMEM((4,) + queries.shape, BF16), dma((2, 4))],
    )(*landed)


def solution(mesh):
    placed = P(("ctx", "head"), None)
    return jax.shard_map(
        per_device,
        mesh=mesh,
        in_specs=(placed,) * 4 + (P(),),
        out_specs=(placed,) * 4,
        check_vma=False,
    )
```
